32 devices in a mesh: blk: 16 (over z, y, core), head: 2 (over x).
Axes of the slice: x: 2, y: 2, z: 4, core: 2. Of those that a mesh axis runs over, the one named last changes fastest.
Arguments:
- queries: bfloat16 [3072, 4096], P(('blk', 'head'))
- key_rows: bfloat16 [3072, 1024], P(('blk', 'head'))
- value_rows: bfloat16 [3072, 1024], P(('blk', 'head')), may hold values from -6 to 6
- visit_ids: int32 [3072], replicated, may hold values from 0 to 3, as said below
- span_order: int32 [16], replicated, may hold values from 0 to 15, each once
Outputs:
- attended: bfloat16 [3072, 4096], P(('blk', 'head'))
The draws below stay inside these ranges and needn't reach their ends.
Inputs may be any that keep to these rules, and one draw needn't show every extreme that they name: `visit_ids`: visit ids never fall along time; every one of the 4 visits has events and begins at an even position. `span_order`: each block index holds a different block of 192 consecutive events.
All inputs are finite; a program needn't handle non-finite values.
Results may differ from the reference program's by a relative error of at most 0.0049.
Values may be sent and summed in bfloat16 or wider, within the bound.
A program may use at most 64 MiB of HBM per device.

```python
import jax
import jax.numpy as jnp
from jax import lax

HEADS = 32
KV_HEADS = 8
HEAD_DIM = 128
BLK_ROWS = 192
VISITS = 4
LEN = 3072
SPANS = 16
KV_WIDTH = 1024


def drawn_rows(key):
    query_key = jax.random.fold_in(key, 11)
    key_key = jax.random.fold_in(key, 12)
    query_base = jnp.clip(jax.random.normal(query_key, (LEN, HEADS, HEAD_DIM), jnp.float32), -6.0, 6.0)
    key_base = jnp.clip(jax.random.normal(key_key, (LEN, KV_HEADS, HEAD_DIM), jnp.float32), -6.0, 6.0)
    return (query_base.reshape(LEN, HEADS * HEAD_DIM), key_base.reshape(LEN, KV_HEADS * HEAD_DIM))


def draw_queries(key, part):
    return drawn_rows(key)[0].astype(jnp.bfloat16)


def draw_key_rows(key, part):
    return drawn_rows(key)[1].astype(jnp.bfloat16)


def draw_visit_ids(key, part):
    pair_count = LEN // 2
    cuts = jax.random.permutation(jax.random.fold_in(key, 21), pair_count - 1)[:VISITS - 1] + 1
    pair_index = jnp.arange(pair_count, dtype=jnp.int32)
    pair_visit = jnp.sum((pair_index[:, None] >= cuts[None, :]).astype(jnp.int32), axis=1)
    return jnp.repeat(pair_visit, 2).astype(jnp.int32)


def block_levels(stream_key, shape, shards, smallest, top_value):
    factor_of, own = 1.0, jax.random.fold_in(stream_key, 6)
    for axis_at, parts in shards:
        steps = jnp.exp(jax.random.uniform(jax.random.fold_in(own, axis_at), (parts,), jnp.float32, smallest / len(shards), top_value / len(shards)))
        factor_of = factor_of * jnp.repeat(steps, shape[axis_at] // parts).reshape([-1 if axis == axis_at else 1 for axis in range(len(shape))])
    return factor_of


def gaussian(stream_key, shape, width, most, shards=(), kind=jnp.bfloat16):
    result = width * jax.random.normal(stream_key, shape, jnp.float32)
    if shards:
        result = result * block_levels(stream_key, shape, shards, -0.22, 0.18)
    return jnp.clip(result, -most, most).astype(kind)


def setup_inputs(seed: int = 0) -> dict:
    splits = jax.random.split(jax.random.key(seed), 6)
    queries = draw_queries(jax.random.fold_in(splits[5], 71), 0)
    key_rows = draw_key_rows(jax.random.fold_in(splits[5], 71), 0)
    value_rows = gaussian(splits[2], (LEN, KV_WIDTH), 1.0, 6.0, ((0, 32),))
    visit_ids = draw_visit_ids(jax.random.fold_in(splits[5], 71), 0)
    span_order = jax.random.permutation(splits[4], SPANS).astype(jnp.int32)
    return {"queries": queries, "key_rows": key_rows, "value_rows": value_rows, "visit_ids": visit_ids, "span_order": span_order}


def natural_positions(span_order):
    every_row = jnp.arange(LEN, dtype=jnp.int32)
    return (span_order[every_row // BLK_ROWS] * BLK_ROWS + every_row % BLK_ROWS).astype(jnp.int32)


def reference(queries, key_rows, value_rows, visit_ids, span_order):
    group_size = HEADS // KV_HEADS
    score_scale = HEAD_DIM ** -0.5
    positions = natural_positions(span_order)
    visits = jnp.take(visit_ids, positions)
    query_heads = queries.reshape(LEN, KV_HEADS, group_size, HEAD_DIM)
    key_heads = key_rows.reshape(LEN, KV_HEADS, HEAD_DIM)
    value_heads = value_rows.reshape(LEN, KV_HEADS, HEAD_DIM)
    block_count = LEN // BLK_ROWS

    def one_block(pair_index):
        block_index = pair_index // KV_HEADS
        head_index = pair_index % KV_HEADS
        first_row = (block_index * BLK_ROWS).astype(jnp.int32)
        query_block = lax.dynamic_slice_in_dim(query_heads, first_row, BLK_ROWS, 0)
        query_block = lax.dynamic_index_in_dim(query_block, head_index, 1, keepdims=False)
        key_head = lax.dynamic_index_in_dim(key_heads, head_index, 1, keepdims=False)
        value_head = lax.dynamic_index_in_dim(value_heads, head_index, 1, keepdims=False)
        scores = jnp.einsum("qgd,kd->qgk", query_block.astype(jnp.float32), key_head.astype(jnp.float32)) * score_scale
        query_pos = lax.dynamic_slice_in_dim(positions, first_row, BLK_ROWS, 0)
        query_visit = lax.dynamic_slice_in_dim(visits, first_row, BLK_ROWS, 0)
        allowed = (positions[None, :] <= query_pos[:, None]) & (visits[None, :] == query_visit[:, None])
        masked = jnp.where(allowed[:, None, :], scores, -jnp.inf)
        row_max = jnp.max(masked, axis=-1, keepdims=True)
        weights = jnp.where(allowed[:, None, :], jnp.exp(masked - row_max), 0.0)
        total = jnp.sum(weights, axis=-1, keepdims=True)
        rounded = lax.optimization_barrier(weights.astype(jnp.bfloat16)).astype(jnp.float32)
        mixed = jnp.einsum("qgk,kd->qgd", rounded, value_head.astype(jnp.float32)) / total
        return mixed.astype(jnp.bfloat16)

    results = lax.map(one_block, jnp.arange(block_count * KV_HEADS, dtype=jnp.int32))
    results = results.reshape(block_count, KV_HEADS, BLK_ROWS, group_size, HEAD_DIM)
    results = jnp.transpose(results, (0, 2, 1, 3, 4))
    return results.reshape(LEN, HEADS * HEAD_DIM)
```

```python
import functools

import jax
import jax.numpy as jnp
from jax import lax
from jax.experimental import pallas as pl
from jax.experimental.pallas import tpu as pltpu
from jax.sharding import PartitionSpec as P

HEADS = 32
KV_HEADS = 8
HEAD_DIM = 128
VISITS = 4
GROUP = HEADS // KV_HEADS
LOG2E = 1.4426950408889634

MESH = pl.DeviceIdType.MESH

masked_score = -1e30


def span_of(cycle_positions, span_order):
    table_index = jnp.arange(span_order.shape[0], dtype=jnp.int32)
    picked = jnp.where(cycle_positions[:, None] == table_index[None, :], span_order[None, :], 0)
    return jnp.sum(picked, axis=1)


def gathered_body(queries, key_rows, value_rows, visit_ids, span_order):
    head_queries, head_keys, head_values = (
        lax.all_to_all(queries, "head", split_axis=1, concat_axis=0, tiled=True),
        lax.all_to_all(key_rows, "head", split_axis=1, concat_axis=0, tiled=True),
        lax.all_to_all(value_rows, "head", split_axis=1, concat_axis=0, tiled=True),
    )
    row_count = head_queries.shape[0]
    group_size = HEADS // KV_HEADS
    local_heads = head_keys.shape[1] // HEAD_DIM
    grouped = head_queries.reshape(row_count, local_heads, group_size, HEAD_DIM)
    cycle_index = lax.axis_index("blk")
    score_scale = HEAD_DIM ** (-0.5)
    my_span = span_of(jnp.full((1,), cycle_index, jnp.int32), span_order)[0]
    query_pos = my_span * row_count + jnp.arange(row_count, dtype=jnp.int32)
    query_visit = jnp.take(visit_ids, query_pos)

    def attend(state_now, kv_block, first_row):
        width = kv_block.shape[1]
        global_rows = first_row + jnp.arange(width, dtype=jnp.int32)
        key_pos = (
            span_of(global_rows // row_count, span_order) * row_count + global_rows % row_count
        )
        key_visit = jnp.take(visit_ids, key_pos)
        allowed = (key_pos[None, :] <= query_pos[:, None]) & (
            key_visit[None, :] == query_visit[:, None]
        )
        run_max, run_total, run_acc = state_now
        key_heads = kv_block[0].reshape(width, local_heads, HEAD_DIM)
        value_heads = kv_block[1].reshape(width, local_heads, HEAD_DIM)
        scores = (
            jnp.einsum("qhgd,khd->qhgk", grouped, key_heads, preferred_element_type=jnp.float32)
            * score_scale
        )
        mask_wide = allowed[:, None, None, :]
        masked = jnp.where(mask_wide, scores, masked_score)
        new_max = jnp.maximum(run_max, jnp.max(masked, axis=-1))
        factor = jnp.exp(run_max - new_max)
        weights = jnp.where(mask_wide, jnp.exp(masked - new_max[..., None]), 0.0)
        new_total = run_total * factor + jnp.sum(weights, axis=-1)
        new_acc = run_acc * factor[..., None] + jnp.einsum(
            "qhgk,khd->qhgd",
            weights.astype(jnp.bfloat16),
            value_heads,
            preferred_element_type=jnp.float32,
        )
        return (new_max, new_total, new_acc)

    kv_local = jnp.stack([head_keys, head_values])
    stat_shape = (row_count, local_heads, group_size)
    initial = (
        jnp.full(stat_shape, masked_score, jnp.float32),
        jnp.zeros(stat_shape, jnp.float32),
        jnp.zeros(stat_shape + (HEAD_DIM,), jnp.float32),
    )
    part_rows = lax.all_gather(kv_local, "blk", axis=1, tiled=True)
    width = part_rows.shape[1]
    step_rows = width
    step_rows = 4 * row_count

    def inner(turn_index, state_in):
        offset = turn_index * step_rows
        sub_block = lax.dynamic_slice_in_dim(part_rows, offset, step_rows, 1)
        return attend(state_in, sub_block, offset)

    state_now = lax.fori_loop(0, width // step_rows, inner, initial)
    run_max, run_total, run_acc = state_now
    attended_local = (run_acc / run_total[..., None]).astype(jnp.bfloat16)
    attended_local = attended_local.reshape(row_count, local_heads * group_size * HEAD_DIM)
    return lax.all_to_all(attended_local, "head", split_axis=0, concat_axis=1, tiled=True)


def fused_kernel(
    dims, q_ref, k_ref, v_ref, visit_ref, span_ref, out_ref,
    kv, qs, outs, bias,
    kv_recv, y_send, core_send, z_send, x_send, x_recv, own_sem, out_send, out_recv, out_own,
):
    nz, nh, rows, phases = dims
    nblk = 4 * nz
    block = nh * rows
    keys = nblk * block
    me = lax.axis_index("blk")
    x = lax.axis_index("head")
    z, y, core = me // 4, (me // 2) % 2, me % 2

    def index_of(z_at, y_at, core_at):
        return z_at * 4 + y_at * 2 + core_at

    z_peers = [lax.rem(z + step, nz) for step in range(1, nz)]
    z_ids = [index_of(zp, y, core) for zp in z_peers]
    y_id = index_of(z, 1 - y, core)
    core_id = index_of(z, y, 1 - core)
    x_peers = [lax.rem(x + step, nh) for step in range(1, nh)]

    barrier = pltpu.get_barrier_semaphore()
    for blk in z_ids + [y_id, core_id]:
        pl.semaphore_signal(barrier, inc=1, device_id=(blk, x), device_id_type=MESH)
    for xp in x_peers:
        pl.semaphore_signal(barrier, inc=1, device_id=(me, xp), device_id_type=MESH)

    def sources(p, to):
        kv_at = pl.multiple_of((to * phases + p) * HEAD_DIM, HEAD_DIM)
        q_at = pl.multiple_of((to * phases + p) * GROUP * HEAD_DIM, GROUP * HEAD_DIM)
        return (
            k_ref.at[:, pl.ds(kv_at, HEAD_DIM)],
            v_ref.at[:, pl.ds(kv_at, HEAD_DIM)],
            q_ref.at[:, pl.ds(q_at, GROUP * HEAD_DIM)],
        )

    def landing(p, source):
        row = pl.multiple_of(me * block + source * rows, 16)
        return (
            kv.at[p, 0, pl.ds(row, rows), :],
            kv.at[p, 1, pl.ds(row, rows), :],
            qs.at[p, source],
        )

    def own_copies(p):
        return [
            pltpu.make_async_copy(src, dst, own_sem.at[p, kind])
            for kind, (src, dst) in enumerate(zip(sources(p, x), landing(p, x)))
        ]

    def x_copies(p, kinds):
        result = []
        for step, xp in enumerate(x_peers):
            from_refs, to_refs = sources(p, xp), landing(p, x)
            for kind in kinds:
                result.append(
                    pltpu.make_async_remote_copy(
                        src_ref=from_refs[kind], dst_ref=to_refs[kind],
                        send_sem=x_send.at[p, step, kind], recv_sem=x_recv.at[p, step, kind],
                        device_id=(me, xp), device_id_type=MESH,
                    )
                )
        return result

    def block_ref(p, blk):
        return kv.at[p, :, pl.ds(pl.multiple_of(blk * block, 16), block), :]

    def gather_copy(p, blk, send_sem, target):
        return pltpu.make_async_remote_copy(
            src_ref=block_ref(p, blk), dst_ref=block_ref(p, blk),
            send_sem=send_sem, recv_sem=kv_recv.at[p, blk],
            device_id=(target, x), device_id_type=MESH,
        )

    sent = []

    def send(copy):
        copy.start()
        sent.append(copy)

    def await_block(p, blk):
        gather_copy(p, blk, y_send.at[p, 0], y_id).wait_recv()

    def start_own(p):
        for copy in own_copies(p)[:2]:
            copy.wait()
        for copy in x_copies(p, (0, 1)):
            copy.wait()
        send(gather_copy(p, me, y_send.at[p, 0], y_id))
        for step, blk in enumerate(z_ids):
            send(gather_copy(p, me, z_send.at[p, step], blk))
        send(gather_copy(p, me, core_send.at[p, 0], core_id))

    def forward_z(p, step):
        blk = index_of(lax.rem(z + nz - 1 - step, nz), y, core)
        await_block(p, blk)
        send(gather_copy(p, blk, y_send.at[p, 1 + step], y_id))
        send(gather_copy(p, blk, core_send.at[p, 1 + step], core_id))

    def forward_y(p):
        for step in range(nz):
            blk = index_of(lax.rem(z + nz - step, nz), 1 - y, core)
            await_block(p, blk)
            send(gather_copy(p, blk, core_send.at[p, nz + step], core_id))

    def await_core(p):
        for side in (y, 1 - y):
            for step in range(nz):
                await_block(p, index_of(lax.rem(z + nz - step, nz), side, 1 - core))

    for p in range(phases):
        for copy in own_copies(p):
            copy.start()

    query_pos = span_ref[me] * block + lax.broadcasted_iota(jnp.int32, (block, 1), 0)
    first = jnp.zeros((block, 1), jnp.int32)
    visits = visit_ref[...]
    for visit in range(1, VISITS):
        begin = jnp.sum(jnp.where(visits < visit, 1.0, 0.0), axis=1, keepdims=True)
        begin = jnp.sum(begin, axis=0, keepdims=True).astype(jnp.int32)
        first = jnp.where(begin <= query_pos, jnp.maximum(first, begin), first)
    lane = lax.broadcasted_iota(jnp.int32, (1, 2 * block), 1)
    for pair in range(nblk // 2):
        key_pos = jnp.where(
            lane < block,
            span_ref[2 * pair] * block + lane,
            span_ref[2 * pair + 1] * block + (lane - block),
        )
        allowed = (key_pos <= query_pos) & (key_pos >= first)
        bias[:, 2 * block * pair : 2 * block * (pair + 1)] = jnp.where(allowed, 0.0, -jnp.inf)

    pl.semaphore_wait(barrier, nz + 1 + nh - 1)

    for copy in x_copies(0, (0, 1, 2)):
        copy.start()
    for p in range(1, min(2, phases)):
        for copy in x_copies(p, (0, 1, 2)):
            copy.start()
    start_own(0)

    chunk = next(size for size in (512, 384, 256, 128) if keys % size == 0)
    batch = 2
    scale = HEAD_DIM**-0.5 * LOG2E
    lowest = -3.0e38

    def compute(p, part):
        at = part * batch
        query = jnp.concatenate(
            [
                jnp.concatenate([qs[p, h, :, g * HEAD_DIM : (g + 1) * HEAD_DIM] for h in range(nh)], axis=0)
                for g in range(at, at + batch)
            ],
            axis=0,
        )

        def step(index, state):
            run_max, run_acc = state
            start = pl.multiple_of(index * chunk, chunk)
            key = kv[p, 0, pl.ds(start, chunk), :]
            value = kv[p, 1, pl.ds(start, chunk), :]
            extended = jnp.concatenate([value, jnp.ones_like(value)], axis=1)
            score = lax.dot_general(
                query, key, (((1,), (1,)), ((), ())), preferred_element_type=jnp.float32
            )
            mask = bias[:, pl.ds(start, chunk)]
            shifted = jnp.concatenate(
                [score[i * block : (i + 1) * block] * scale + mask for i in range(batch)], axis=0
            )
            new_max = jnp.maximum(run_max, jnp.max(shifted, axis=1, keepdims=True))
            weight = jnp.exp2(shifted - new_max).astype(jnp.bfloat16)
            factor = jnp.exp2(run_max - new_max)
            new_acc = run_acc * factor + jnp.dot(
                weight, extended, preferred_element_type=jnp.float32
            )
            return new_max, new_acc

        initial = (
            jnp.full((batch * block, 1), lowest, jnp.float32),
            jnp.zeros((batch * block, 2 * HEAD_DIM), jnp.float32),
        )
        _, acc = lax.fori_loop(0, keys // chunk, step, initial)
        result = (acc[:, :HEAD_DIM] / acc[:, HEAD_DIM:]).astype(jnp.bfloat16)
        for i in range(batch):
            for h in range(nh):
                first_row = i * block + h * rows
                outs[p, h, :, (at + i) * HEAD_DIM : (at + i + 1) * HEAD_DIM] = result[
                    first_row : first_row + rows
                ]

    width = GROUP * HEAD_DIM

    def out_copies(p):
        place = out_ref.at[:, pl.ds(pl.multiple_of((x * phases + p) * width, width), width)]
        copies = [pltpu.make_async_copy(outs.at[p, x], place, out_own.at[p])]
        for step, xp in enumerate(x_peers):
            copies.append(
                pltpu.make_async_remote_copy(
                    src_ref=outs.at[p, xp], dst_ref=place,
                    send_sem=out_send.at[p, step], recv_sem=out_recv.at[p, step],
                    device_id=(me, xp), device_id_type=MESH,
                )
            )
        return copies

    for step in range(nz - 1):
        forward_z(0, step)
    for p in range(phases):
        more = p + 1 < phases
        if more:
            start_own(p + 1)
        if p + 2 < phases:
            for copy in x_copies(p + 2, (0, 1, 2)):
                copy.start()
        forward_y(p)
        own_copies(p)[2].wait()
        for copy in x_copies(p, (2,)):
            copy.wait()
        await_core(p)
        parts = GROUP // batch
        passed = 0
        for part in range(parts):
            compute(p, part)
            upto = (nz - 1) * (part + 1) // parts
            while more and passed < upto:
                forward_z(p + 1, passed)
                passed += 1
        for copy in out_copies(p):
            copy.start()
    for p in range(phases):
        for copy in out_copies(p):
            copy.wait()
    for copy in sent:
        copy.wait_send()


def fused_body(nblk, nh, queries, key_rows, value_rows, visit_ids, span_order):
    rows = queries.shape[0]
    block = rows * nh
    phases = KV_HEADS // nh
    nz = nblk // 4
    dma = pltpu.SemaphoreType.DMA
    any_spec = pl.BlockSpec(memory_space=pl.ANY)
    return pl.pallas_call(
        functools.partial(fused_kernel, (nz, nh, rows, phases)),
        out_shape=jax.ShapeDtypeStruct(queries.shape, jnp.bfloat16),
        in_specs=[
            any_spec,
            any_spec,
            any_spec,
            pl.BlockSpec(memory_space=pltpu.VMEM),
            pl.BlockSpec(memory_space=pltpu.SMEM),
        ],
        out_specs=pl.BlockSpec(memory_space=pltpu.VMEM),
        scratch_shapes=[
            pltpu.VMEM((phases, 2, nblk * block, HEAD_DIM), jnp.bfloat16),
            pltpu.VMEM((phases, nh, rows, GROUP * HEAD_DIM), jnp.bfloat16),
            pltpu.VMEM((phases, nh, rows, GROUP * HEAD_DIM), jnp.bfloat16),
            pltpu.VMEM((block, nblk * block), jnp.float32),
            dma((phases, nblk)),
            dma((phases, nz)),
            dma((phases, 2 * nz)),
            dma((phases, nz - 1)),
            dma((phases, nh - 1, 3)),
            dma((phases, nh - 1, 3)),
            dma((phases, 3)),
            dma((phases, nh - 1)),
            dma((phases, nh - 1)),
            dma((phases,)),
        ],
        compiler_params=pltpu.CompilerParams(
            collective_id=0, has_side_effects=True, vmem_limit_bytes=48 * 2**20
        ),
        name="visit_attention",
    )(queries, key_rows, value_rows, visit_ids.reshape(-1, 128), span_order)


def solution(mesh):
    placed = (
        P(("blk", "head"), None),
        P(("blk", "head"), None),
        P(("blk", "head"), None),
        P(),
        P(),
    )
    nblk, nh = mesh.shape["blk"], mesh.shape["head"]

    def body(queries, *rest):
        if queries.shape[0] % 16 == 0 and nblk % 4 == 0 and KV_HEADS % nh == 0:
            return fused_body(nblk, nh, queries, *rest)
        return gathered_body(queries, *rest)

    return jax.shard_map(
        body, mesh=mesh, in_specs=placed, out_specs=P(("blk", "head"), None), check_vma=False
    )
```

```python
import functools

import jax
import jax.numpy as jnp
from jax import lax
from jax.experimental import pallas as pl
from jax.experimental.pallas import tpu as pltpu
from jax.sharding import PartitionSpec as P

HEADS = 32
KV_HEADS = 8
HEAD_DIM = 128
VISITS = 4
GROUP = HEADS // KV_HEADS
LOG2E = 1.4426950408889634

MESH = pl.DeviceIdType.MESH

masked_score = -1e30


def span_of(cycle_positions, span_order):
    table_index = jnp.arange(span_order.shape[0], dtype=jnp.int32)
    picked = jnp.where(cycle_positions[:, None] == table_index[None, :], span_order[None, :], 0)
    return jnp.sum(picked, axis=1)


def gathered_body(queries, key_rows, value_rows, visit_ids, span_order):
    head_queries, head_keys, head_values = (
        lax.all_to_all(queries, "head", split_axis=1, concat_axis=0, tiled=True),
        lax.all_to_all(key_rows, "head", split_axis=1, concat_axis=0, tiled=True),
        lax.all_to_all(value_rows, "head", split_axis=1, concat_axis=0, tiled=True),
    )
    row_count = head_queries.shape[0]
    group_size = HEADS // KV_HEADS
    local_heads = head_keys.shape[1] // HEAD_DIM
    grouped = head_queries.reshape(row_count, local_heads, group_size, HEAD_DIM)
    cycle_index = lax.axis_index("blk")
    score_scale = HEAD_DIM ** (-0.5)
    my_span = span_of(jnp.full((1,), cycle_index, jnp.int32), span_order)[0]
    query_pos = my_span * row_count + jnp.arange(row_count, dtype=jnp.int32)
    query_visit = jnp.take(visit_ids, query_pos)

    def attend(state_now, kv_block, first_row):
        width = kv_block.shape[1]
        global_rows = first_row + jnp.arange(width, dtype=jnp.int32)
        key_pos = (
            span_of(global_rows // row_count, span_order) * row_count + global_rows % row_count
        )
        key_visit = jnp.take(visit_ids, key_pos)
        allowed = (key_pos[None, :] <= query_pos[:, None]) & (
            key_visit[None, :] == query_visit[:, None]
        )
        run_max, run_total, run_acc = state_now
        key_heads = kv_block[0].reshape(width, local_heads, HEAD_DIM)
        value_heads = kv_block[1].reshape(width, local_heads, HEAD_DIM)
        scores = (
            jnp.einsum("qhgd,khd->qhgk", grouped, key_heads, preferred_element_type=jnp.float32)
            * score_scale
        )
        mask_wide = allowed[:, None, None, :]
        masked = jnp.where(mask_wide, scores, masked_score)
        new_max = jnp.maximum(run_max, jnp.max(masked, axis=-1))
        factor = jnp.exp(run_max - new_max)
        weights = jnp.where(mask_wide, jnp.exp(masked - new_max[..., None]), 0.0)
        new_total = run_total * factor + jnp.sum(weights, axis=-1)
        new_acc = run_acc * factor[..., None] + jnp.einsum(
            "qhgk,khd->qhgd",
            weights.astype(jnp.bfloat16),
            value_heads,
            preferred_element_type=jnp.float32,
        )
        return (new_max, new_total, new_acc)

    kv_local = jnp.stack([head_keys, head_values])
    stat_shape = (row_count, local_heads, group_size)
    initial = (
        jnp.full(stat_shape, masked_score, jnp.float32),
        jnp.zeros(stat_shape, jnp.float32),
        jnp.zeros(stat_shape + (HEAD_DIM,), jnp.float32),
    )
    part_rows = lax.all_gather(kv_local, "blk", axis=1, tiled=True)
    width = part_rows.shape[1]
    step_rows = width
    step_rows = 4 * row_count

    def inner(turn_index, state_in):
        offset = turn_index * step_rows
        sub_block = lax.dynamic_slice_in_dim(part_rows, offset, step_rows, 1)
        return attend(state_in, sub_block, offset)

    state_now = lax.fori_loop(0, width // step_rows, inner, initial)
    run_max, run_total, run_acc = state_now
    attended_local = (run_acc / run_total[..., None]).astype(jnp.bfloat16)
    attended_local = attended_local.reshape(row_count, local_heads * group_size * HEAD_DIM)
    return lax.all_to_all(attended_local, "head", split_axis=0, concat_axis=1, tiled=True)


def fused_kernel(
    dims, q_ref, k_ref, v_ref, visit_ref, span_ref, out_ref,
    kv, qs, outs, bias,
    kv_recv, y_send, core_send, z_send, x_send, x_recv, own_sem, out_send, out_recv, out_own,
):
    nz, nh, rows, phases = dims
    nblk = 4 * nz
    block = nh * rows
    keys = nblk * block
    me = lax.axis_index("blk")
    x = lax.axis_index("head")
    z, y, core = me // 4, (me // 2) % 2, me % 2

    def index_of(z_at, y_at, core_at):
        return z_at * 4 + y_at * 2 + core_at

    z_peers = [lax.rem(z + step, nz) for step in range(1, nz)]
    z_ids = [index_of(zp, y, core) for zp in z_peers]
    y_id = index_of(z, 1 - y, core)
    core_id = index_of(z, y, 1 - core)
    x_peers = [lax.rem(x + step, nh) for step in range(1, nh)]

    barrier = pltpu.get_barrier_semaphore()
    for blk in z_ids + [y_id, core_id]:
        pl.semaphore_signal(barrier, inc=1, device_id=(blk, x), device_id_type=MESH)
    for xp in x_peers:
        pl.semaphore_signal(barrier, inc=1, device_id=(me, xp), device_id_type=MESH)

    def sources(p, to):
        kv_at = pl.multiple_of((to * phases + p) * HEAD_DIM, HEAD_DIM)
        q_at = pl.multiple_of((to * phases + p) * GROUP * HEAD_DIM, GROUP * HEAD_DIM)
        return (
            k_ref.at[:, pl.ds(kv_at, HEAD_DIM)],
            v_ref.at[:, pl.ds(kv_at, HEAD_DIM)],
            q_ref.at[:, pl.ds(q_at, GROUP * HEAD_DIM)],
        )

    def landing(p, source):
        row = pl.multiple_of(me * block + source * rows, 16)
        return (
            kv.at[p, 0, pl.ds(row, rows), :],
            kv.at[p, 1, pl.ds(row, rows), :],
            qs.at[p, source],
        )

    def own_copies(p, kinds=3, first_kind=0):
        pairs = list(zip(sources(p, x), landing(p, x)))
        return [
            pltpu.make_async_copy(*pairs[kind], own_sem.at[p, kind])
            for kind in range(first_kind, kinds)
        ]

    def x_copies(p, kinds):
        result = []
        for step, xp in enumerate(x_peers):
            from_refs, to_refs = sources(p, xp), landing(p, x)
            for kind in kinds:
                result.append(
                    pltpu.make_async_remote_copy(
                        src_ref=from_refs[kind], dst_ref=to_refs[kind],
                        send_sem=x_send.at[p, step, kind], recv_sem=x_recv.at[p, step, kind],
                        device_id=(me, xp), device_id_type=MESH,
                    )
                )
        return result

    def block_ref(p, blk):
        return kv.at[p, :, pl.ds(pl.multiple_of(blk * block, 16), block), :]

    def gather_copy(p, blk, send_sem, target):
        return pltpu.make_async_remote_copy(
            src_ref=block_ref(p, blk), dst_ref=block_ref(p, blk),
            send_sem=send_sem, recv_sem=kv_recv.at[p, blk],
            device_id=(target, x), device_id_type=MESH,
        )

    def await_block(p, blk):
        gather_copy(p, blk, y_send.at[p, 0], y_id).wait_recv()

    def own_sends(p):
        copies = [gather_copy(p, me, y_send.at[p, 0], y_id)]
        for step, blk in enumerate(z_ids):
            copies.append(gather_copy(p, me, z_send.at[p, step], blk))
        copies.append(gather_copy(p, me, core_send.at[p, 0], core_id))
        return copies

    def start_own(p):
        for copy in own_copies(p, 2):
            copy.wait()
        for copy in x_copies(p, (0, 1)):
            copy.wait()
        for copy in own_sends(p):
            copy.start()

    def z_block(step):
        return index_of(lax.rem(z + nz - 1 - step, nz), y, core)

    def z_forwards(p, step):
        blk = z_block(step)
        return [
            gather_copy(p, blk, y_send.at[p, 1 + step], y_id),
            gather_copy(p, blk, core_send.at[p, 1 + step], core_id),
        ]

    def forward_z(p, step):
        await_block(p, z_block(step))
        for copy in z_forwards(p, step):
            copy.start()

    def y_block(step):
        return index_of(lax.rem(z + nz - step, nz), 1 - y, core)

    def y_forward(p, step):
        return gather_copy(p, y_block(step), core_send.at[p, nz + step], core_id)

    def forward_y(p, step):
        await_block(p, y_block(step))
        y_forward(p, step).start()

    def await_core(p):
        for side in (y, 1 - y):
            for step in range(nz):
                await_block(p, index_of(lax.rem(z + nz - step, nz), side, 1 - core))

    for p in range(phases):
        for copy in own_copies(p):
            copy.start()

    query_pos = span_ref[me] * block + lax.broadcasted_iota(jnp.int32, (block, 1), 0)
    first = jnp.zeros((block, 1), jnp.int32)
    visits = visit_ref[...]
    for visit in range(1, VISITS):
        begin = jnp.sum(jnp.where(visits < visit, 1.0, 0.0), axis=1, keepdims=True)
        begin = jnp.sum(begin, axis=0, keepdims=True).astype(jnp.int32)
        first = jnp.where(begin <= query_pos, jnp.maximum(first, begin), first)
    lane = lax.broadcasted_iota(jnp.int32, (1, 2 * block), 1)
    for pair in range(nblk // 2):
        key_pos = jnp.where(
            lane < block,
            span_ref[2 * pair] * block + lane,
            span_ref[2 * pair + 1] * block + (lane - block),
        )
        allowed = (key_pos <= query_pos) & (key_pos >= first)
        bias[:, 2 * block * pair : 2 * block * (pair + 1)] = jnp.where(allowed, 0.0, -jnp.inf)

    pl.semaphore_wait(barrier, nz + 1 + nh - 1)

    for p in range(phases):
        for copy in x_copies(p, (0, 1)):
            copy.start()
    for p in range(phases):
        for copy in x_copies(p, (2,)):
            copy.start()

    chunk = next(size for size in (512, 384, 256, 128) if keys % size == 0)
    batch = 2
    scale = HEAD_DIM**-0.5 * LOG2E
    lowest = -3.0e38

    def compute(p, part, events):
        at = part * batch
        query = jnp.concatenate(
            [
                jnp.concatenate([qs[p, h, :, g * HEAD_DIM : (g + 1) * HEAD_DIM] for h in range(nh)], axis=0)
                for g in range(at, at + batch)
            ],
            axis=0,
        )

        def step(index, state):
            for slot, event in events:
                pl.when(index == slot)(event)
            run_max, run_acc = state
            start = pl.multiple_of(index * chunk, chunk)
            key = kv[p, 0, pl.ds(start, chunk), :]
            value = kv[p, 1, pl.ds(start, chunk), :]
            extended = jnp.concatenate([value, jnp.ones_like(value)], axis=1)
            score = lax.dot_general(
                query, key, (((1,), (1,)), ((), ())), preferred_element_type=jnp.float32
            )
            mask = bias[:, pl.ds(start, chunk)]
            shifted = jnp.concatenate(
                [score[i * block : (i + 1) * block] * scale + mask for i in range(batch)], axis=0
            )
            new_max = jnp.maximum(run_max, jnp.max(shifted, axis=1, keepdims=True))
            weight = jnp.exp2(shifted - new_max).astype(jnp.bfloat16)
            factor = jnp.exp2(run_max - new_max)
            new_acc = run_acc * factor + jnp.dot(
                weight, extended, preferred_element_type=jnp.float32
            )
            return new_max, new_acc

        initial = (
            jnp.full((batch * block, 1), lowest, jnp.float32),
            jnp.zeros((batch * block, 2 * HEAD_DIM), jnp.float32),
        )
        _, acc = lax.fori_loop(0, keys // chunk, step, initial)
        result = (acc[:, :HEAD_DIM] / acc[:, HEAD_DIM:]).astype(jnp.bfloat16)
        for i in range(batch):
            for h in range(nh):
                first_row = i * block + h * rows
                outs[p, h, :, (at + i) * HEAD_DIM : (at + i + 1) * HEAD_DIM] = result[
                    first_row : first_row + rows
                ]

    width = batch * HEAD_DIM
    parts = GROUP // batch

    def out_copies(p, part):
        at = pl.multiple_of(((x * phases + p) * parts + part) * width, width)
        place = out_ref.at[:, pl.ds(at, width)]
        held = pl.ds(part * width, width)
        copies = [pltpu.make_async_copy(outs.at[p, x, :, held], place, out_own.at[p, part])]
        for step, xp in enumerate(x_peers):
            copies.append(
                pltpu.make_async_remote_copy(
                    src_ref=outs.at[p, xp, :, held], dst_ref=place,
                    send_sem=out_send.at[p, part, step], recv_sem=out_recv.at[p, part, step],
                    device_id=(me, xp), device_id_type=MESH,
                )
            )
        return copies

    chunks = keys // chunk
    slots = chunks * parts

    def events_of(p):
        events = [functools.partial(forward_y, p, 0)]
        events += [functools.partial(forward_z, p, step) for step in range(nz - 1)]
        return [(min(slots - 1, (k + 1) * slots // (len(events) + 1)), e) for k, e in enumerate(events)]

    for p in range(min(2, phases)):
        start_own(p)
    for step in range(nz - 1):
        forward_z(0, step)
    forward_y(0, 0)
    for p in range(phases):
        if p + 2 < phases:
            start_own(p + 2)
        for step in range(1, nz):
            forward_y(p, step)
        for copy in own_copies(p, 3, 2):
            copy.wait()
        for copy in x_copies(p, (2,)):
            copy.wait()
        await_core(p)
        events = events_of(p + 1) if p + 1 < phases else []
        for part in range(parts):
            low = part * chunks
            compute(p, part, [(slot - low, e) for slot, e in events if low <= slot < low + chunks])
            for copy in out_copies(p, part):
                copy.start()
    for p in range(phases):
        for part in range(parts):
            for copy in out_copies(p, part):
                copy.wait()
        for copy in own_sends(p):
            copy.wait_send()
        for step in range(nz - 1):
            for copy in z_forwards(p, step):
                copy.wait_send()
        for step in range(nz):
            y_forward(p, step).wait_send()


def fused_body(nblk, nh, queries, key_rows, value_rows, visit_ids, span_order):
    rows = queries.shape[0]
    block = rows * nh
    phases = KV_HEADS // nh
    nz = nblk // 4
    dma = pltpu.SemaphoreType.DMA
    any_spec = pl.BlockSpec(memory_space=pl.ANY)
    return pl.pallas_call(
        functools.partial(fused_kernel, (nz, nh, rows, phases)),
        out_shape=jax.ShapeDtypeStruct(queries.shape, jnp.bfloat16),
        in_specs=[
            any_spec,
            any_spec,
            any_spec,
            pl.BlockSpec(memory_space=pltpu.VMEM),
            pl.BlockSpec(memory_space=pltpu.SMEM),
        ],
        out_specs=pl.BlockSpec(memory_space=pltpu.VMEM),
        scratch_shapes=[
            pltpu.VMEM((phases, 2, nblk * block, HEAD_DIM), jnp.bfloat16),
            pltpu.VMEM((phases, nh, rows, GROUP * HEAD_DIM), jnp.bfloat16),
            pltpu.VMEM((phases, nh, rows, GROUP * HEAD_DIM), jnp.bfloat16),
            pltpu.VMEM((block, nblk * block), jnp.float32),
            dma((phases, nblk)),
            dma((phases, nz)),
            dma((phases, 2 * nz)),
            dma((phases, nz - 1)),
            dma((phases, nh - 1, 3)),
            dma((phases, nh - 1, 3)),
            dma((phases, 3)),
            dma((phases, GROUP, nh - 1)),
            dma((phases, GROUP, nh - 1)),
            dma((phases, GROUP)),
        ],
        compiler_params=pltpu.CompilerParams(
            collective_id=0, has_side_effects=True, vmem_limit_bytes=60 * 2**20
        ),
        name="visit_attention",
    )(queries, key_rows, value_rows, visit_ids.reshape(-1, 128), span_order)


def solution(mesh):
    placed = (
        P(("blk", "head"), None),
        P(("blk", "head"), None),
        P(("blk", "head"), None),
        P(),
        P(),
    )
    nblk, nh = mesh.shape["blk"], mesh.shape["head"]

    def body(queries, *rest):
        if queries.shape[0] % 16 == 0 and nblk % 4 == 0 and KV_HEADS % nh == 0:
            return fused_body(nblk, nh, queries, *rest)
        return gathered_body(queries, *rest)

    return jax.shard_map(
        body, mesh=mesh, in_specs=placed, out_specs=P(("blk", "head"), None), check_vma=False
    )
```

```python
import functools

import jax
import jax.numpy as jnp
from jax import lax
from jax.experimental import pallas as pl
from jax.experimental.pallas import tpu as pltpu
from jax.sharding import PartitionSpec as P

HEADS = 32
KV_HEADS = 8
HEAD_DIM = 128
VISITS = 4
GROUP = HEADS // KV_HEADS

MESH = pl.DeviceIdType.MESH

masked_score = -1e30


def span_of(cycle_positions, span_order):
    table_index = jnp.arange(span_order.shape[0], dtype=jnp.int32)
    picked = jnp.where(cycle_positions[:, None] == table_index[None, :], span_order[None, :], 0)
    return jnp.sum(picked, axis=1)


def gathered_body(queries, key_rows, value_rows, visit_ids, span_order):
    head_queries, head_keys, head_values = (
        lax.all_to_all(queries, "head", split_axis=1, concat_axis=0, tiled=True),
        lax.all_to_all(key_rows, "head", split_axis=1, concat_axis=0, tiled=True),
        lax.all_to_all(value_rows, "head", split_axis=1, concat_axis=0, tiled=True),
    )
    row_count = head_queries.shape[0]
    group_size = HEADS // KV_HEADS
    local_heads = head_keys.shape[1] // HEAD_DIM
    grouped = head_queries.reshape(row_count, local_heads, group_size, HEAD_DIM)
    cycle_index = lax.axis_index("blk")
    score_scale = HEAD_DIM ** (-0.5)
    my_span = span_of(jnp.full((1,), cycle_index, jnp.int32), span_order)[0]
    query_pos = my_span * row_count + jnp.arange(row_count, dtype=jnp.int32)
    query_visit = jnp.take(visit_ids, query_pos)

    def attend(state_now, kv_block, first_row):
        width = kv_block.shape[1]
        global_rows = first_row + jnp.arange(width, dtype=jnp.int32)
        key_pos = (
            span_of(global_rows // row_count, span_order) * row_count + global_rows % row_count
        )
        key_visit = jnp.take(visit_ids, key_pos)
        allowed = (key_pos[None, :] <= query_pos[:, None]) & (
            key_visit[None, :] == query_visit[:, None]
        )
        run_max, run_total, run_acc = state_now
        key_heads = kv_block[0].reshape(width, local_heads, HEAD_DIM)
        value_heads = kv_block[1].reshape(width, local_heads, HEAD_DIM)
        scores = (
            jnp.einsum("qhgd,khd->qhgk", grouped, key_heads, preferred_element_type=jnp.float32)
            * score_scale
        )
        mask_wide = allowed[:, None, None, :]
        masked = jnp.where(mask_wide, scores, masked_score)
        new_max = jnp.maximum(run_max, jnp.max(masked, axis=-1))
        factor = jnp.exp(run_max - new_max)
        weights = jnp.where(mask_wide, jnp.exp(masked - new_max[..., None]), 0.0)
        new_total = run_total * factor + jnp.sum(weights, axis=-1)
        new_acc = run_acc * factor[..., None] + jnp.einsum(
            "qhgk,khd->qhgd",
            weights.astype(jnp.bfloat16),
            value_heads,
            preferred_element_type=jnp.float32,
        )
        return (new_max, new_total, new_acc)

    kv_local = jnp.stack([head_keys, head_values])
    stat_shape = (row_count, local_heads, group_size)
    initial = (
        jnp.full(stat_shape, masked_score, jnp.float32),
        jnp.zeros(stat_shape, jnp.float32),
        jnp.zeros(stat_shape + (HEAD_DIM,), jnp.float32),
    )
    part_rows = lax.all_gather(kv_local, "blk", axis=1, tiled=True)
    width = part_rows.shape[1]
    step_rows = width
    step_rows = 4 * row_count

    def inner(turn_index, state_in):
        offset = turn_index * step_rows
        sub_block = lax.dynamic_slice_in_dim(part_rows, offset, step_rows, 1)
        return attend(state_in, sub_block, offset)

    state_now = lax.fori_loop(0, width // step_rows, inner, initial)
    run_max, run_total, run_acc = state_now
    attended_local = (run_acc / run_total[..., None]).astype(jnp.bfloat16)
    attended_local = attended_local.reshape(row_count, local_heads * group_size * HEAD_DIM)
    return lax.all_to_all(attended_local, "head", split_axis=0, concat_axis=1, tiled=True)


def gather_kernel(
    dims, q_ref, k_ref, v_ref, kv, qs,
    kv_recv, y_send, core_send, z_send, x_send, x_recv, own_sem,
):
    nz, nh, rows, phases = dims
    nblk = 4 * nz
    block = nh * rows
    keys = nblk * block
    me = lax.axis_index("blk")
    x = lax.axis_index("head")
    z, y, core = me // 4, (me // 2) % 2, me % 2

    def index_of(z_at, y_at, core_at):
        return z_at * 4 + y_at * 2 + core_at

    z_peers = [lax.rem(z + step, nz) for step in range(1, nz)]
    z_ids = [index_of(zp, y, core) for zp in z_peers]
    y_id = index_of(z, 1 - y, core)
    core_id = index_of(z, y, 1 - core)
    x_peers = [lax.rem(x + step, nh) for step in range(1, nh)]

    barrier = pltpu.get_barrier_semaphore()
    for blk in z_ids + [y_id, core_id]:
        pl.semaphore_signal(barrier, inc=1, device_id=(blk, x), device_id_type=MESH)
    for xp in x_peers:
        pl.semaphore_signal(barrier, inc=1, device_id=(me, xp), device_id_type=MESH)

    def sources(p, to):
        kv_at = pl.multiple_of((to * phases + p) * HEAD_DIM, HEAD_DIM)
        q_at = pl.multiple_of((to * phases + p) * GROUP * HEAD_DIM, GROUP * HEAD_DIM)
        return (
            k_ref.at[:, pl.ds(kv_at, HEAD_DIM)],
            v_ref.at[:, pl.ds(kv_at, HEAD_DIM)],
            q_ref.at[:, pl.ds(q_at, GROUP * HEAD_DIM)],
        )

    def landing(p, source):
        row = pl.multiple_of(me * block + source * rows, 16)
        return (
            kv.at[p, 0, pl.ds(row, rows), :],
            kv.at[p, 1, pl.ds(row, rows), :],
            qs.at[p, source],
        )

    def own_copies(p, kinds=3, first_kind=0):
        pairs = list(zip(sources(p, x), landing(p, x)))
        return [
            pltpu.make_async_copy(*pairs[kind], own_sem.at[p, kind])
            for kind in range(first_kind, kinds)
        ]

    def x_copies(p, kinds):
        result = []
        for step, xp in enumerate(x_peers):
            from_refs, to_refs = sources(p, xp), landing(p, x)
            for kind in kinds:
                result.append(
                    pltpu.make_async_remote_copy(
                        src_ref=from_refs[kind], dst_ref=to_refs[kind],
                        send_sem=x_send.at[p, step, kind], recv_sem=x_recv.at[p, step, kind],
                        device_id=(me, xp), device_id_type=MESH,
                    )
                )
        return result

    def block_ref(p, blk):
        return kv.at[p, :, pl.ds(pl.multiple_of(blk * block, 16), block), :]

    def gather_copy(p, blk, send_sem, target):
        return pltpu.make_async_remote_copy(
            src_ref=block_ref(p, blk), dst_ref=block_ref(p, blk),
            send_sem=send_sem, recv_sem=kv_recv.at[p, blk],
            device_id=(target, x), device_id_type=MESH,
        )

    def await_block(p, blk):
        gather_copy(p, blk, y_send.at[p, 0], y_id).wait_recv()

    def own_sends(p):
        copies = [gather_copy(p, me, y_send.at[p, 0], y_id)]
        for step, blk in enumerate(z_ids):
            copies.append(gather_copy(p, me, z_send.at[p, step], blk))
        copies.append(gather_copy(p, me, core_send.at[p, 0], core_id))
        return copies

    def start_own(p):
        for copy in own_copies(p, 2):
            copy.wait()
        for copy in x_copies(p, (0, 1)):
            copy.wait()
        for copy in own_sends(p):
            copy.start()

    def z_block(step):
        return index_of(lax.rem(z + nz - 1 - step, nz), y, core)

    def z_forwards(p, step):
        blk = z_block(step)
        return [
            gather_copy(p, blk, y_send.at[p, 1 + step], y_id),
            gather_copy(p, blk, core_send.at[p, 1 + step], core_id),
        ]

    def forward_z(p, step):
        await_block(p, z_block(step))
        for copy in z_forwards(p, step):
            copy.start()

    def y_block(step):
        return index_of(lax.rem(z + nz - step, nz), 1 - y, core)

    def y_forward(p, step):
        return gather_copy(p, y_block(step), core_send.at[p, nz + step], core_id)

    def forward_y(p, step):
        await_block(p, y_block(step))
        y_forward(p, step).start()

    def await_core(p):
        for side in (y, 1 - y):
            for step in range(nz):
                await_block(p, index_of(lax.rem(z + nz - step, nz), side, 1 - core))

    for p in range(phases):
        for copy in own_copies(p):
            copy.start()

    pl.semaphore_wait(barrier, nz + 1 + nh - 1)

    for p in range(phases):
        for copy in x_copies(p, (0, 1)):
            copy.start()
    for p in range(phases):
        for copy in x_copies(p, (2,)):
            copy.start()

    for p in range(min(2, phases)):
        start_own(p)
    for p in range(phases):
        if p + 2 < phases:
            start_own(p + 2)
        forward_y(p, 0)
        for step in range(nz - 1):
            forward_z(p, step)
        for step in range(1, nz):
            forward_y(p, step)
    for p in range(phases):
        await_core(p)
        for copy in own_copies(p, 3, 2):
            copy.wait()
        for copy in x_copies(p, (2,)):
            copy.wait()
        for copy in own_sends(p):
            copy.wait_send()
        for step in range(nz - 1):
            for copy in z_forwards(p, step):
                copy.wait_send()
        for step in range(nz):
            y_forward(p, step).wait_send()


def attend_kernel(dims, meta_ref, order_ref, visit_ref, qs, kv, outs):
    nz, nh, rows, phases = dims
    block = nh * rows
    scale = HEAD_DIM**-0.5
    lowest = -3.0e38
    my_span, low_span = meta_ref[0], meta_ref[1]

    query_pos = my_span * block + lax.broadcasted_iota(jnp.int32, (block, 1), 0)
    first = jnp.zeros((block, 1), jnp.int32)
    visits = visit_ref[...]
    for visit in range(1, VISITS):
        begin = jnp.sum(jnp.where(visits < visit, 1.0, 0.0), axis=1, keepdims=True)
        begin = jnp.sum(begin, axis=0, keepdims=True).astype(jnp.int32)
        first = jnp.where(begin <= query_pos, jnp.maximum(first, begin), first)
    lane = lax.broadcasted_iota(jnp.int32, (1, block), 1)

    def one_head(p, carry):
        query = jnp.concatenate(
            [
                jnp.concatenate([qs[p, h, :, g * HEAD_DIM : (g + 1) * HEAD_DIM] for h in range(nh)], axis=0)
                for g in range(GROUP)
            ],
            axis=0,
        )

        def step(span, state):
            run_max, run_acc = state
            start = pl.multiple_of(order_ref[span] * block, 64)
            key = kv[p, 0, pl.ds(start, block), :]
            value = kv[p, 1, pl.ds(start, block), :]
            extended = jnp.concatenate([value, jnp.ones_like(value)], axis=1)
            score = lax.dot_general(
                query, key, (((1,), (1,)), ((), ())), preferred_element_type=jnp.float32
            )
            key_pos = span * block + lane
            mask = jnp.where((key_pos <= query_pos) & (key_pos >= first), 0.0, -jnp.inf)
            shifted = jnp.concatenate(
                [score[i * block : (i + 1) * block] * scale + mask for i in range(GROUP)], axis=0
            )
            new_max = jnp.maximum(run_max, jnp.max(shifted, axis=1, keepdims=True))
            weight = jnp.exp(shifted - new_max).astype(jnp.bfloat16)
            factor = jnp.exp(run_max - new_max)
            new_acc = run_acc * factor + jnp.dot(
                weight, extended, preferred_element_type=jnp.float32
            )
            return new_max, new_acc

        initial = (
            jnp.full((GROUP * block, 1), lowest, jnp.float32),
            jnp.zeros((GROUP * block, 2 * HEAD_DIM), jnp.float32),
        )
        _, acc = lax.fori_loop(low_span, my_span + 1, step, initial)
        result = (acc[:, :HEAD_DIM] / acc[:, HEAD_DIM:]).astype(jnp.bfloat16)
        for i in range(GROUP):
            for h in range(nh):
                first_row = i * block + h * rows
                outs[p, h, :, i * HEAD_DIM : (i + 1) * HEAD_DIM] = result[
                    first_row : first_row + rows
                ]
        return carry

    lax.fori_loop(0, phases, one_head, 0)


def exchange_kernel(dims, outs, out_ref, out_own, out_send, out_recv):
    nz, nh, rows, phases = dims
    me = lax.axis_index("blk")
    x = lax.axis_index("head")
    x_peers = [lax.rem(x + step, nh) for step in range(1, nh)]
    barrier = pltpu.get_barrier_semaphore()
    for xp in x_peers:
        pl.semaphore_signal(barrier, inc=1, device_id=(me, xp), device_id_type=MESH)
    pl.semaphore_wait(barrier, nh - 1)
    width = GROUP * HEAD_DIM
    copies = []
    for p in range(phases):
        at = pl.multiple_of((x * phases + p) * width, width)
        place = out_ref.at[:, pl.ds(at, width)]
        copies.append(pltpu.make_async_copy(outs.at[p, x], place, out_own.at[p]))
        for step, xp in enumerate(x_peers):
            copies.append(
                pltpu.make_async_remote_copy(
                    src_ref=outs.at[p, xp], dst_ref=place,
                    send_sem=out_send.at[p, step], recv_sem=out_recv.at[p, step],
                    device_id=(me, xp), device_id_type=MESH,
                )
            )
    for copy in copies:
        copy.start()
    for copy in copies:
        copy.wait()


def fused_body(nblk, nh, queries, key_rows, value_rows, visit_ids, span_order):
    rows = queries.shape[0]
    block = rows * nh
    phases = KV_HEADS // nh
    nz = nblk // 4
    dma = pltpu.SemaphoreType.DMA
    any_spec = pl.BlockSpec(memory_space=pl.ANY)
    dims = (nz, nh, rows, phases)
    keys = nblk * block
    kv, qs = pl.pallas_call(
        functools.partial(gather_kernel, dims),
        out_shape=(
            jax.ShapeDtypeStruct((phases, 2, keys, HEAD_DIM), jnp.bfloat16),
            jax.ShapeDtypeStruct((phases, nh, rows, GROUP * HEAD_DIM), jnp.bfloat16),
        ),
        in_specs=[any_spec, any_spec, any_spec],
        out_specs=(any_spec, any_spec),
        scratch_shapes=[
            dma((phases, nblk)),
            dma((phases, nz)),
            dma((phases, 2 * nz)),
            dma((phases, nz - 1)),
            dma((phases, nh - 1, 3)),
            dma((phases, nh - 1, 3)),
            dma((phases, 3)),
        ],
        compiler_params=pltpu.CompilerParams(
            collective_id=0, has_side_effects=True, vmem_limit_bytes=60 * 2**20
        ),
        name="gather_heads",
    )(queries, key_rows, value_rows)
    blocks = jnp.arange(nblk, dtype=jnp.int32)
    order = jnp.sum(jnp.where(span_order[None, :] == blocks[:, None], blocks[None, :], 0), axis=1)
    my_span = jnp.sum(jnp.where(blocks == lax.axis_index("blk"), span_order, 0))
    begins = [jnp.sum((visit_ids < visit).astype(jnp.int32)) for visit in range(1, VISITS)]
    low = jnp.int32(0)
    for begin in begins:
        low = jnp.where(begin <= my_span * block, jnp.maximum(low, begin), low)
    meta = jnp.stack([my_span, low // block]).astype(jnp.int32)
    smem = pl.BlockSpec(memory_space=pltpu.SMEM)
    vmem = pl.BlockSpec(memory_space=pltpu.VMEM)
    outs = pl.pallas_call(
        functools.partial(attend_kernel, dims),
        out_shape=jax.ShapeDtypeStruct((phases, nh, rows, GROUP * HEAD_DIM), jnp.bfloat16),
        in_specs=[smem, smem, vmem, vmem, vmem],
        out_specs=vmem,
        compiler_params=pltpu.CompilerParams(vmem_limit_bytes=40 * 2**20),
        name="attend_heads",
    )(meta, order.astype(jnp.int32), visit_ids.reshape(-1, 128), qs, kv)
    return pl.pallas_call(
        functools.partial(exchange_kernel, dims),
        out_shape=jax.ShapeDtypeStruct(queries.shape, jnp.bfloat16),
        in_specs=[any_spec],
        out_specs=any_spec,
        scratch_shapes=[dma((phases,)), dma((phases, nh - 1)), dma((phases, nh - 1))],
        compiler_params=pltpu.CompilerParams(collective_id=1, has_side_effects=True),
        name="exchange_rows",
    )(outs)


def solution(mesh):
    placed = (
        P(("blk", "head"), None),
        P(("blk", "head"), None),
        P(("blk", "head"), None),
        P(),
        P(),
    )
    nblk, nh = mesh.shape["blk"], mesh.shape["head"]

    def body(queries, *rest):
        if queries.shape[0] % 16 == 0 and nblk % 4 == 0 and KV_HEADS % nh == 0:
            return fused_body(nblk, nh, queries, *rest)
        return gathered_body(queries, *rest)

    return jax.shard_map(
        body, mesh=mesh, in_specs=placed, out_specs=P(("blk", "head"), None), check_vma=False
    )
```

```python
import functools

import jax
import jax.numpy as jnp
from jax import lax
from jax.experimental import pallas as pl
from jax.experimental.pallas import tpu as pltpu
from jax.sharding import PartitionSpec as P

HEADS = 32
KV_HEADS = 8
HEAD_DIM = 128
VISITS = 4
GROUP = HEADS // KV_HEADS

MESH = pl.DeviceIdType.MESH

masked_score = -1e30


def span_of(cycle_positions, span_order):
    table_index = jnp.arange(span_order.shape[0], dtype=jnp.int32)
    picked = jnp.where(cycle_positions[:, None] == table_index[None, :], span_order[None, :], 0)
    return jnp.sum(picked, axis=1)


def gathered_body(queries, key_rows, value_rows, visit_ids, span_order):
    head_queries, head_keys, head_values = (
        lax.all_to_all(queries, "head", split_axis=1, concat_axis=0, tiled=True),
        lax.all_to_all(key_rows, "head", split_axis=1, concat_axis=0, tiled=True),
        lax.all_to_all(value_rows, "head", split_axis=1, concat_axis=0, tiled=True),
    )
    row_count = head_queries.shape[0]
    group_size = HEADS // KV_HEADS
    local_heads = head_keys.shape[1] // HEAD_DIM
    grouped = head_queries.reshape(row_count, local_heads, group_size, HEAD_DIM)
    cycle_index = lax.axis_index("blk")
    score_scale = HEAD_DIM ** (-0.5)
    my_span = span_of(jnp.full((1,), cycle_index, jnp.int32), span_order)[0]
    query_pos = my_span * row_count + jnp.arange(row_count, dtype=jnp.int32)
    query_visit = jnp.take(visit_ids, query_pos)

    def attend(state_now, kv_block, first_row):
        width = kv_block.shape[1]
        global_rows = first_row + jnp.arange(width, dtype=jnp.int32)
        key_pos = (
            span_of(global_rows // row_count, span_order) * row_count + global_rows % row_count
        )
        key_visit = jnp.take(visit_ids, key_pos)
        allowed = (key_pos[None, :] <= query_pos[:, None]) & (
            key_visit[None, :] == query_visit[:, None]
        )
        run_max, run_total, run_acc = state_now
        key_heads = kv_block[0].reshape(width, local_heads, HEAD_DIM)
        value_heads = kv_block[1].reshape(width, local_heads, HEAD_DIM)
        scores = (
            jnp.einsum("qhgd,khd->qhgk", grouped, key_heads, preferred_element_type=jnp.float32)
            * score_scale
        )
        mask_wide = allowed[:, None, None, :]
        masked = jnp.where(mask_wide, scores, masked_score)
        new_max = jnp.maximum(run_max, jnp.max(masked, axis=-1))
        factor = jnp.exp(run_max - new_max)
        weights = jnp.where(mask_wide, jnp.exp(masked - new_max[..., None]), 0.0)
        new_total = run_total * factor + jnp.sum(weights, axis=-1)
        new_acc = run_acc * factor[..., None] + jnp.einsum(
            "qhgk,khd->qhgd",
            weights.astype(jnp.bfloat16),
            value_heads,
            preferred_element_type=jnp.float32,
        )
        return (new_max, new_total, new_acc)

    kv_local = jnp.stack([head_keys, head_values])
    stat_shape = (row_count, local_heads, group_size)
    initial = (
        jnp.full(stat_shape, masked_score, jnp.float32),
        jnp.zeros(stat_shape, jnp.float32),
        jnp.zeros(stat_shape + (HEAD_DIM,), jnp.float32),
    )
    part_rows = lax.all_gather(kv_local, "blk", axis=1, tiled=True)
    width = part_rows.shape[1]
    step_rows = width
    step_rows = 4 * row_count

    def inner(turn_index, state_in):
        offset = turn_index * step_rows
        sub_block = lax.dynamic_slice_in_dim(part_rows, offset, step_rows, 1)
        return attend(state_in, sub_block, offset)

    state_now = lax.fori_loop(0, width // step_rows, inner, initial)
    run_max, run_total, run_acc = state_now
    attended_local = (run_acc / run_total[..., None]).astype(jnp.bfloat16)
    attended_local = attended_local.reshape(row_count, local_heads * group_size * HEAD_DIM)
    return lax.all_to_all(attended_local, "head", split_axis=0, concat_axis=1, tiled=True)


def fused_kernel(
    dims, q_ref, k_ref, v_ref, visit_ref, span_ref, out_ref,
    kv, qs, outs, bias,
    kv_recv, y_send, core_send, z_send, x_send, x_recv, own_sem, out_send, out_recv, out_own,
):
    nz, nh, rows, phases = dims
    nblk = 4 * nz
    block = nh * rows
    keys = nblk * block
    me = lax.axis_index("blk")
    x = lax.axis_index("head")
    z, y, core = me // 4, (me // 2) % 2, me % 2

    def index_of(z_at, y_at, core_at):
        return z_at * 4 + y_at * 2 + core_at

    z_peers = [lax.rem(z + step, nz) for step in range(1, nz)]
    z_ids = [index_of(zp, y, core) for zp in z_peers]
    y_id = index_of(z, 1 - y, core)
    core_id = index_of(z, y, 1 - core)
    x_peers = [lax.rem(x + step, nh) for step in range(1, nh)]

    barrier = pltpu.get_barrier_semaphore()
    for blk in z_ids + [y_id, core_id]:
        pl.semaphore_signal(barrier, inc=1, device_id=(blk, x), device_id_type=MESH)
    for xp in x_peers:
        pl.semaphore_signal(barrier, inc=1, device_id=(me, xp), device_id_type=MESH)

    def sources(p, to):
        kv_at = pl.multiple_of((to * phases + p) * HEAD_DIM, HEAD_DIM)
        q_at = pl.multiple_of((to * phases + p) * GROUP * HEAD_DIM, GROUP * HEAD_DIM)
        return (
            k_ref.at[:, pl.ds(kv_at, HEAD_DIM)],
            v_ref.at[:, pl.ds(kv_at, HEAD_DIM)],
            q_ref.at[:, pl.ds(q_at, GROUP * HEAD_DIM)],
        )

    def landing(p, source):
        row = pl.multiple_of(me * block + source * rows, 16)
        return (
            kv.at[p, 0, pl.ds(row, rows), :],
            kv.at[p, 1, pl.ds(row, rows), :],
            qs.at[p, source],
        )

    def own_copies(p, kinds=3, first_kind=0):
        pairs = list(zip(sources(p, x), landing(p, x)))
        return [
            pltpu.make_async_copy(*pairs[kind], own_sem.at[p, kind])
            for kind in range(first_kind, kinds)
        ]

    def x_copies(p, kinds):
        result = []
        for step, xp in enumerate(x_peers):
            from_refs, to_refs = sources(p, xp), landing(p, x)
            for kind in kinds:
                result.append(
                    pltpu.make_async_remote_copy(
                        src_ref=from_refs[kind], dst_ref=to_refs[kind],
                        send_sem=x_send.at[p, step, kind], recv_sem=x_recv.at[p, step, kind],
                        device_id=(me, xp), device_id_type=MESH,
                    )
                )
        return result

    def block_ref(p, blk):
        return kv.at[p, :, pl.ds(pl.multiple_of(blk * block, 16), block), :]

    def gather_copy(p, blk, send_sem, target):
        return pltpu.make_async_remote_copy(
            src_ref=block_ref(p, blk), dst_ref=block_ref(p, blk),
            send_sem=send_sem, recv_sem=kv_recv.at[p, blk],
            device_id=(target, x), device_id_type=MESH,
        )

    def await_block(p, blk):
        gather_copy(p, blk, y_send.at[p, 0], y_id).wait_recv()

    def own_sends(p):
        copies = [gather_copy(p, me, y_send.at[p, 0], y_id)]
        for step, blk in enumerate(z_ids):
            copies.append(gather_copy(p, me, z_send.at[p, step], blk))
        copies.append(gather_copy(p, me, core_send.at[p, 0], core_id))
        return copies

    def start_own(p):
        for copy in own_copies(p, 2):
            copy.wait()
        for copy in x_copies(p, (0, 1)):
            copy.wait()
        for copy in own_sends(p):
            copy.start()

    def z_block(step):
        return index_of(lax.rem(z + nz - 1 - step, nz), y, core)

    def z_forwards(p, step):
        blk = z_block(step)
        return [
            gather_copy(p, blk, y_send.at[p, 1 + step], y_id),
            gather_copy(p, blk, core_send.at[p, 1 + step], core_id),
        ]

    def forward_z(p, step):
        await_block(p, z_block(step))
        for copy in z_forwards(p, step):
            copy.start()

    def y_block(step):
        return index_of(lax.rem(z + nz - step, nz), 1 - y, core)

    def y_forward(p, step):
        return gather_copy(p, y_block(step), core_send.at[p, nz + step], core_id)

    def forward_y(p, step):
        await_block(p, y_block(step))
        y_forward(p, step).start()

    def await_core(p):
        for side in (y, 1 - y):
            for step in range(nz):
                await_block(p, index_of(lax.rem(z + nz - step, nz), side, 1 - core))

    for p in range(phases):
        for copy in own_copies(p):
            copy.start()

    columns = GROUP * block
    column = lax.broadcasted_iota(jnp.int32, (1, columns), 1)
    offset = column
    for g in range(1, GROUP):
        offset = jnp.where(column >= g * block, column - g * block, offset)
    query_pos = span_ref[me] * block + offset
    first = jnp.zeros((1, columns), jnp.int32)
    visits = visit_ref[...]
    for visit in range(1, VISITS):
        begin = jnp.sum(jnp.where(visits < visit, 1.0, 0.0), axis=1, keepdims=True)
        begin = jnp.sum(begin, axis=0, keepdims=True).astype(jnp.int32)
        first = jnp.where(begin <= query_pos, jnp.maximum(first, begin), first)
    row = lax.broadcasted_iota(jnp.int32, (block, 1), 0)

    def mask_block(blk, carry):
        key_pos = span_ref[blk] * block + row
        allowed = (key_pos <= query_pos) & (key_pos >= first)
        bias[pl.ds(pl.multiple_of(blk * block, 16), block), :] = jnp.where(allowed, 0.0, -jnp.inf)
        return carry

    lax.fori_loop(0, nblk, mask_block, 0)

    pl.semaphore_wait(barrier, nz + 1 + nh - 1)

    for p in range(phases):
        for copy in x_copies(p, (0, 1)):
            copy.start()
    for p in range(phases):
        for copy in x_copies(p, (2,)):
            copy.start()

    chunk = next(size for size in (512, 384, 256, 128) if keys % size == 0)
    batch = GROUP
    scale = HEAD_DIM**-0.5
    lowest = -3.0e38

    def compute(p, part, events):
        at = part * batch
        query = jnp.concatenate(
            [
                jnp.concatenate([qs[p, h, :, g * HEAD_DIM : (g + 1) * HEAD_DIM] for h in range(nh)], axis=0)
                for g in range(at, at + batch)
            ],
            axis=0,
        )

        def step(index, state):
            for slot, event in events:
                pl.when(index == slot)(event)
            run_max, run_acc = state
            start = pl.multiple_of(index * chunk, chunk)
            key = kv[p, 0, pl.ds(start, chunk), :]
            value = kv[p, 1, pl.ds(start, chunk), :]
            extended = jnp.concatenate(
                [jnp.transpose(value), jnp.ones((16, chunk), jnp.bfloat16)], axis=0
            )
            score = lax.dot_general(
                key, query, (((1,), (1,)), ((), ())), preferred_element_type=jnp.float32
            )
            shifted = score * scale + bias[pl.ds(start, chunk), :]
            new_max = jnp.maximum(run_max, jnp.max(shifted, axis=0, keepdims=True))
            weight = jnp.exp(shifted - new_max).astype(jnp.bfloat16)
            factor = jnp.exp(run_max - new_max)
            new_acc = run_acc * factor + jnp.dot(
                extended, weight, preferred_element_type=jnp.float32
            )
            return new_max, new_acc

        initial = (
            jnp.full((1, columns), lowest, jnp.float32),
            jnp.zeros((HEAD_DIM + 16, columns), jnp.float32),
        )
        _, acc = lax.fori_loop(0, keys // chunk, step, initial)
        result = jnp.transpose(acc[:HEAD_DIM] / acc[HEAD_DIM : HEAD_DIM + 1]).astype(jnp.bfloat16)
        for i in range(batch):
            for h in range(nh):
                first_row = i * block + h * rows
                outs[p, h, :, (at + i) * HEAD_DIM : (at + i + 1) * HEAD_DIM] = result[
                    first_row : first_row + rows
                ]

    width = batch * HEAD_DIM
    parts = GROUP // batch

    def out_copies(p, part):
        at = pl.multiple_of(((x * phases + p) * parts + part) * width, width)
        place = out_ref.at[:, pl.ds(at, width)]
        held = pl.ds(part * width, width)
        copies = [pltpu.make_async_copy(outs.at[p, x, :, held], place, out_own.at[p, part])]
        for step, xp in enumerate(x_peers):
            copies.append(
                pltpu.make_async_remote_copy(
                    src_ref=outs.at[p, xp, :, held], dst_ref=place,
                    send_sem=out_send.at[p, part, step], recv_sem=out_recv.at[p, part, step],
                    device_id=(me, xp), device_id_type=MESH,
                )
            )
        return copies

    chunks = keys // chunk
    slots = chunks * parts

    def events_of(p):
        events = [functools.partial(forward_y, p, 0)]
        events += [functools.partial(forward_z, p, step) for step in range(nz - 1)]
        return [(min(slots - 1, (k + 1) * slots // (len(events) + 1)), e) for k, e in enumerate(events)]

    for p in range(min(2, phases)):
        start_own(p)
    for step in range(nz - 1):
        forward_z(0, step)
    forward_y(0, 0)
    for p in range(phases):
        if p + 2 < phases:
            start_own(p + 2)
        for step in range(1, nz):
            forward_y(p, step)
        for copy in own_copies(p, 3, 2):
            copy.wait()
        for copy in x_copies(p, (2,)):
            copy.wait()
        await_core(p)
        events = events_of(p + 1) if p + 1 < phases else []
        for part in range(parts):
            low = part * chunks
            compute(p, part, [(slot - low, e) for slot, e in events if low <= slot < low + chunks])
            for copy in out_copies(p, part):
                copy.start()
    for p in range(phases):
        for part in range(parts):
            for copy in out_copies(p, part):
                copy.wait()
        for copy in own_sends(p):
            copy.wait_send()
        for step in range(nz - 1):
            for copy in z_forwards(p, step):
                copy.wait_send()
        for step in range(nz):
            y_forward(p, step).wait_send()


def fused_body(nblk, nh, queries, key_rows, value_rows, visit_ids, span_order):
    rows = queries.shape[0]
    block = rows * nh
    phases = KV_HEADS // nh
    nz = nblk // 4
    dma = pltpu.SemaphoreType.DMA
    any_spec = pl.BlockSpec(memory_space=pl.ANY)
    return pl.pallas_call(
        functools.partial(fused_kernel, (nz, nh, rows, phases)),
        out_shape=jax.ShapeDtypeStruct(queries.shape, jnp.bfloat16),
        in_specs=[
            any_spec,
            any_spec,
            any_spec,
            pl.BlockSpec(memory_space=pltpu.VMEM),
            pl.BlockSpec(memory_space=pltpu.SMEM),
        ],
        out_specs=pl.BlockSpec(memory_space=pltpu.VMEM),
        scratch_shapes=[
            pltpu.VMEM((phases, 2, nblk * block, HEAD_DIM), jnp.bfloat16),
            pltpu.VMEM((phases, nh, rows, GROUP * HEAD_DIM), jnp.bfloat16),
            pltpu.VMEM((phases, nh, rows, GROUP * HEAD_DIM), jnp.bfloat16),
            pltpu.VMEM((nblk * block, GROUP * block), jnp.float32),
            dma((phases, nblk)),
            dma((phases, nz)),
            dma((phases, 2 * nz)),
            dma((phases, nz - 1)),
            dma((phases, nh - 1, 3)),
            dma((phases, nh - 1, 3)),
            dma((phases, 3)),
            dma((phases, GROUP, nh - 1)),
            dma((phases, GROUP, nh - 1)),
            dma((phases, GROUP)),
        ],
        compiler_params=pltpu.CompilerParams(
            collective_id=0, has_side_effects=True, vmem_limit_bytes=60 * 2**20
        ),
        name="visit_attention",
    )(queries, key_rows, value_rows, visit_ids.reshape(-1, 128), span_order)


def solution(mesh):
    placed = (
        P(("blk", "head"), None),
        P(("blk", "head"), None),
        P(("blk", "head"), None),
        P(),
        P(),
    )
    nblk, nh = mesh.shape["blk"], mesh.shape["head"]

    def body(queries, *rest):
        if queries.shape[0] % 16 == 0 and nblk % 4 == 0 and KV_HEADS % nh == 0:
            return fused_body(nblk, nh, queries, *rest)
        return gathered_body(queries, *rest)

    return jax.shard_map(
        body, mesh=mesh, in_specs=placed, out_specs=P(("blk", "head"), None), check_vma=False
    )
```

```python
import functools

import jax
import jax.numpy as jnp
from jax import lax
from jax.experimental import pallas as pl
from jax.experimental.pallas import tpu as pltpu
from jax.sharding import PartitionSpec as P

HEADS = 32
KV_HEADS = 8
HEAD_DIM = 128
VISITS = 4
GROUP = HEADS // KV_HEADS

MESH = pl.DeviceIdType.MESH

masked_score = -1e30


def span_of(cycle_positions, span_order):
    table_index = jnp.arange(span_order.shape[0], dtype=jnp.int32)
    picked = jnp.where(cycle_positions[:, None] == table_index[None, :], span_order[None, :], 0)
    return jnp.sum(picked, axis=1)


def gathered_body(queries, key_rows, value_rows, visit_ids, span_order):
    head_queries, head_keys, head_values = (
        lax.all_to_all(queries, "head", split_axis=1, concat_axis=0, tiled=True),
        lax.all_to_all(key_rows, "head", split_axis=1, concat_axis=0, tiled=True),
        lax.all_to_all(value_rows, "head", split_axis=1, concat_axis=0, tiled=True),
    )
    row_count = head_queries.shape[0]
    group_size = HEADS // KV_HEADS
    local_heads = head_keys.shape[1] // HEAD_DIM
    grouped = head_queries.reshape(row_count, local_heads, group_size, HEAD_DIM)
    cycle_index = lax.axis_index("blk")
    score_scale = HEAD_DIM ** (-0.5)
    my_span = span_of(jnp.full((1,), cycle_index, jnp.int32), span_order)[0]
    query_pos = my_span * row_count + jnp.arange(row_count, dtype=jnp.int32)
    query_visit = jnp.take(visit_ids, query_pos)

    def attend(state_now, kv_block, first_row):
        width = kv_block.shape[1]
        global_rows = first_row + jnp.arange(width, dtype=jnp.int32)
        key_pos = (
            span_of(global_rows // row_count, span_order) * row_count + global_rows % row_count
        )
        key_visit = jnp.take(visit_ids, key_pos)
        allowed = (key_pos[None, :] <= query_pos[:, None]) & (
            key_visit[None, :] == query_visit[:, None]
        )
        run_max, run_total, run_acc = state_now
        key_heads = kv_block[0].reshape(width, local_heads, HEAD_DIM)
        value_heads = kv_block[1].reshape(width, local_heads, HEAD_DIM)
        scores = (
            jnp.einsum("qhgd,khd->qhgk", grouped, key_heads, preferred_element_type=jnp.float32)
            * score_scale
        )
        mask_wide = allowed[:, None, None, :]
        masked = jnp.where(mask_wide, scores, masked_score)
        new_max = jnp.maximum(run_max, jnp.max(masked, axis=-1))
        factor = jnp.exp(run_max - new_max)
        weights = jnp.where(mask_wide, jnp.exp(masked - new_max[..., None]), 0.0)
        new_total = run_total * factor + jnp.sum(weights, axis=-1)
        new_acc = run_acc * factor[..., None] + jnp.einsum(
            "qhgk,khd->qhgd",
            weights.astype(jnp.bfloat16),
            value_heads,
            preferred_element_type=jnp.float32,
        )
        return (new_max, new_total, new_acc)

    kv_local = jnp.stack([head_keys, head_values])
    stat_shape = (row_count, local_heads, group_size)
    initial = (
        jnp.full(stat_shape, masked_score, jnp.float32),
        jnp.zeros(stat_shape, jnp.float32),
        jnp.zeros(stat_shape + (HEAD_DIM,), jnp.float32),
    )
    part_rows = lax.all_gather(kv_local, "blk", axis=1, tiled=True)
    width = part_rows.shape[1]
    step_rows = width
    step_rows = 4 * row_count

    def inner(turn_index, state_in):
        offset = turn_index * step_rows
        sub_block = lax.dynamic_slice_in_dim(part_rows, offset, step_rows, 1)
        return attend(state_in, sub_block, offset)

    state_now = lax.fori_loop(0, width // step_rows, inner, initial)
    run_max, run_total, run_acc = state_now
    attended_local = (run_acc / run_total[..., None]).astype(jnp.bfloat16)
    attended_local = attended_local.reshape(row_count, local_heads * group_size * HEAD_DIM)
    return lax.all_to_all(attended_local, "head", split_axis=0, concat_axis=1, tiled=True)


def fused_kernel(
    dims, q_ref, k_ref, v_ref, visit_ref, span_ref, out_ref,
    kv, qs, outs, bias,
    kv_recv, side_recv, y_send, core_send, z_send, side_send, x_send, x_recv, own_sem, out_send, out_recv, out_own,
):
    nz, nh, rows, phases = dims
    nblk = 4 * nz
    block = nh * rows
    keys = nblk * block
    me = lax.axis_index("blk")
    x = lax.axis_index("head")
    z, y, core = me // 4, (me // 2) % 2, me % 2

    def index_of(z_at, y_at, core_at):
        return z_at * 4 + y_at * 2 + core_at

    y_id = index_of(z, 1 - y, core)
    core_id = index_of(z, y, 1 - core)
    x_peers = [lax.rem(x + step, nh) for step in range(1, nh)]
    side_rows = max(16, block // (2 * (nz - 1)) // 16 * 16)

    def next_plane(up):
        return z + 1 if up else z - 1

    def has_next(up):
        return z + 1 < nz if up else z > 0

    barrier = pltpu.get_barrier_semaphore()
    for blk in (y_id, core_id):
        pl.semaphore_signal(barrier, inc=1, device_id=(blk, x), device_id_type=MESH)
    for xp in x_peers:
        pl.semaphore_signal(barrier, inc=1, device_id=(me, xp), device_id_type=MESH)
    for up in (True, False):

        @pl.when(has_next(up))
        def _(up=up):
            target = index_of(next_plane(up), y, core)
            pl.semaphore_signal(barrier, inc=1, device_id=(target, x), device_id_type=MESH)

    def sources(p, to):
        kv_at = pl.multiple_of((to * phases + p) * HEAD_DIM, HEAD_DIM)
        q_at = pl.multiple_of((to * phases + p) * GROUP * HEAD_DIM, GROUP * HEAD_DIM)
        return (
            k_ref.at[:, pl.ds(kv_at, HEAD_DIM)],
            v_ref.at[:, pl.ds(kv_at, HEAD_DIM)],
            q_ref.at[:, pl.ds(q_at, GROUP * HEAD_DIM)],
        )

    def landing(p, source):
        row = pl.multiple_of(me * block + source * rows, 16)
        return (
            kv.at[p, 0, pl.ds(row, rows), :],
            kv.at[p, 1, pl.ds(row, rows), :],
            qs.at[p, source],
        )

    def own_copies(p, kinds=3, first_kind=0):
        pairs = list(zip(sources(p, x), landing(p, x)))
        return [
            pltpu.make_async_copy(*pairs[kind], own_sem.at[p, kind])
            for kind in range(first_kind, kinds)
        ]

    def x_copies(p, kinds):
        result = []
        for step, xp in enumerate(x_peers):
            from_refs, to_refs = sources(p, xp), landing(p, x)
            for kind in kinds:
                result.append(
                    pltpu.make_async_remote_copy(
                        src_ref=from_refs[kind], dst_ref=to_refs[kind],
                        send_sem=x_send.at[p, step, kind], recv_sem=x_recv.at[p, step, kind],
                        device_id=(me, xp), device_id_type=MESH,
                    )
                )
        return result

    def rows_ref(p, blk, first_row, count):
        at = pl.multiple_of(blk * block + first_row, 16)
        return kv.at[p, :, pl.ds(at, count), :]

    def remote(ref, send_sem, recv_sem, target):
        return pltpu.make_async_remote_copy(
            src_ref=ref, dst_ref=ref, send_sem=send_sem, recv_sem=recv_sem,
            device_id=(target, x), device_id_type=MESH,
        )

    def whole_copy(p, blk, send_sem, target):
        return remote(rows_ref(p, blk, 0, block), send_sem, kv_recv.at[p, blk], target)

    def y_copy(p, plane):
        blk = index_of(plane, y, core)
        if plane is z:
            return whole_copy(p, blk, y_send.at[p, plane], y_id)
        ref = rows_ref(p, blk, side_rows, block - side_rows)
        return remote(ref, y_send.at[p, plane], kv_recv.at[p, blk], y_id)

    def core_copy(p, plane, side):
        blk = index_of(plane, y if side == 0 else 1 - y, core)
        return whole_copy(p, blk, core_send.at[p, side, plane], core_id)

    def z_copy(p, plane, up):
        blk, to = index_of(plane, y, core), index_of(next_plane(up), y, core)
        return whole_copy(p, blk, z_send.at[p, int(up), plane], to)

    def side_copy(p, plane, up):
        blk, to = index_of(plane, 1 - y, core), index_of(next_plane(up), y, core)
        ref = rows_ref(p, blk, 0, side_rows)
        return remote(ref, side_send.at[p, int(up), plane], side_recv.at[p, plane], to)

    def await_whole(p, blk):
        whole_copy(p, blk, y_send.at[p, 0], y_id).wait_recv()

    def for_next(make, act):
        for up in (True, False):
            pl.when(has_next(up))(functools.partial(lambda up: act(make(up)), up))

    def start(copy):
        copy.start()

    def finish(copy):
        copy.wait_send()

    def start_own(p):
        for copy in own_copies(p, 2):
            copy.wait()
        for copy in x_copies(p, (0, 1)):
            copy.wait()
        y_copy(p, z).start()
        for_next(lambda up: z_copy(p, z, up), start)
        core_copy(p, z, 0).start()

    def pass_peer(p):
        await_whole(p, index_of(z, 1 - y, core))
        for_next(lambda up: side_copy(p, z, up), start)
        core_copy(p, z, 1).start()

    def from_planes(distance, act):
        for up in (True, False):
            plane = z - distance if up else z + distance
            exists = plane >= 0 if up else plane < nz
            pl.when(exists)(functools.partial(act, plane, up))

    def pass_plane(p, distance):
        def act(plane, up):
            await_whole(p, index_of(plane, y, core))

            @pl.when(has_next(up))
            def _():
                z_copy(p, plane, up).start()

            y_copy(p, plane).start()
            core_copy(p, plane, 0).start()
            remote(
                rows_ref(p, index_of(plane, 1 - y, core), 0, side_rows),
                side_send.at[p, 0, 0], side_recv.at[p, plane], y_id,
            ).wait_recv()

            @pl.when(has_next(up))
            def _():
                side_copy(p, plane, up).start()

        from_planes(distance, act)

    def finish_plane(p, distance):
        def act(plane, up):
            @pl.when(has_next(up))
            def _():
                z_copy(p, plane, up).wait_send()
                side_copy(p, plane, up).wait_send()

            y_copy(p, plane).wait_send()
            core_copy(p, plane, 0).wait_send()

        from_planes(distance, act)

    def plane_at(rank):
        return lax.rem(z + jnp.where(2 * z < nz, rank, nz - rank), nz)

    def pass_far(p, rank):
        plane = plane_at(rank)
        blk = index_of(plane, 1 - y, core)
        remote(
            rows_ref(p, blk, side_rows, block - side_rows),
            y_send.at[p, 0], kv_recv.at[p, blk], y_id,
        ).wait_recv()
        core_copy(p, plane, 1).start()

    for p in range(phases):
        for copy in own_copies(p):
            copy.start()

    columns = GROUP * block
    column = lax.broadcasted_iota(jnp.int32, (1, columns), 1)
    offset = column
    for g in range(1, GROUP):
        offset = jnp.where(column >= g * block, column - g * block, offset)
    query_pos = span_ref[me] * block + offset
    first = jnp.zeros((1, columns), jnp.int32)
    visits = visit_ref[...]
    for visit in range(1, VISITS):
        begin = jnp.sum(jnp.where(visits < visit, 1.0, 0.0), axis=1, keepdims=True)
        begin = jnp.sum(begin, axis=0, keepdims=True).astype(jnp.int32)
        first = jnp.where(begin <= query_pos, jnp.maximum(first, begin), first)
    row = lax.broadcasted_iota(jnp.int32, (block, 1), 0)

    def mask_block(blk, carry):
        key_pos = span_ref[blk] * block + row
        allowed = (key_pos <= query_pos) & (key_pos >= first)
        bias[pl.ds(pl.multiple_of(blk * block, 16), block), :] = jnp.where(allowed, 0.0, -jnp.inf)
        return carry

    lax.fori_loop(0, nblk, mask_block, 0)

    planes_beside = jnp.minimum(z, 1) + jnp.minimum(nz - 1 - z, 1)
    pl.semaphore_wait(barrier, 1 + nh + planes_beside)

    def start_x(p, kinds):
        for copy in x_copies(p, kinds):
            copy.start()

    chunk = 2 * block
    batch = GROUP
    scale = HEAD_DIM**-0.5
    lowest = -3.0e38

    def compute(p, events):
        at = 0
        query = jnp.concatenate(
            [
                jnp.concatenate([qs[p, h, :, g * HEAD_DIM : (g + 1) * HEAD_DIM] for h in range(nh)], axis=0)
                for g in range(at, at + batch)
            ],
            axis=0,
        )

        def step(index, state):
            for slot, event in events:
                pl.when(index == slot)(event)
            run_max, run_acc = state
            plane = plane_at(lax.rem(index, nz))
            chip = plane * 2 + jnp.where(index < nz, y, 1 - y)
            await_whole(p, chip * 2 + 1 - core)
            start = pl.multiple_of(chip * chunk, 128)
            key = kv[p, 0, pl.ds(start, chunk), :]
            value = kv[p, 1, pl.ds(start, chunk), :]
            extended = jnp.concatenate(
                [jnp.transpose(value), jnp.ones((16, chunk), jnp.bfloat16)], axis=0
            )
            score = lax.dot_general(
                key, query, (((1,), (1,)), ((), ())), preferred_element_type=jnp.float32
            )
            shifted = score * scale + bias[pl.ds(start, chunk), :]
            new_max = jnp.maximum(run_max, jnp.max(shifted, axis=0, keepdims=True))
            weight = jnp.exp(shifted - new_max).astype(jnp.bfloat16)
            factor = jnp.exp(run_max - new_max)
            new_acc = run_acc * factor + jnp.dot(
                extended, weight, preferred_element_type=jnp.float32
            )
            return new_max, new_acc

        initial = (
            jnp.full((1, columns), lowest, jnp.float32),
            jnp.zeros((HEAD_DIM + 16, columns), jnp.float32),
        )
        _, acc = lax.fori_loop(0, 2 * nz, step, initial)
        result = jnp.transpose(acc[:HEAD_DIM] / acc[HEAD_DIM : HEAD_DIM + 1]).astype(jnp.bfloat16)
        for i in range(batch):
            for h in range(nh):
                first_row = i * block + h * rows
                outs[p, h, :, (at + i) * HEAD_DIM : (at + i + 1) * HEAD_DIM] = result[
                    first_row : first_row + rows
                ]

    width = GROUP * HEAD_DIM

    def out_copies(p):
        place = out_ref.at[:, pl.ds(pl.multiple_of((x * phases + p) * width, width), width)]
        copies = [pltpu.make_async_copy(outs.at[p, x], place, out_own.at[p])]
        for step, xp in enumerate(x_peers):
            copies.append(
                pltpu.make_async_remote_copy(
                    src_ref=outs.at[p, xp], dst_ref=place,
                    send_sem=out_send.at[p, step], recv_sem=out_recv.at[p, step],
                    device_id=(me, xp), device_id_type=MESH,
                )
            )
        return copies

    def events_of(p):
        events = []
        for rank in range(1, nz):
            events.append((2 * rank, functools.partial(pass_far, p, rank)))
        if p + 1 < phases:
            events.append((0, functools.partial(pass_peer, p + 1)))
            for distance in range(1, nz):
                events.append((2 * distance - 1, functools.partial(pass_plane, p + 1, distance)))
        return events

    start_x(0, (0, 1))
    start_own(0)
    for p in range(1, min(2, phases)):
        start_x(p, (0, 1))
        start_x(p - 1, (2,))
        start_own(p)
    pass_peer(0)
    for p in range(min(2, phases), min(3, phases)):
        start_x(p, (0, 1))
    start_x(min(2, phases) - 1, (2,))
    for distance in range(1, nz):
        pass_plane(0, distance)
    for p in range(phases):
        if p + 2 < phases:
            start_own(p + 2)
            start_x(p + 2, (2,))
            if p + 3 < phases:
                start_x(p + 3, (0, 1))
        for copy in own_copies(p, 3, 2):
            copy.wait()
        for copy in x_copies(p, (2,)):
            copy.wait()
        compute(p, events_of(p))
        for copy in out_copies(p):
            copy.start()
    for p in range(phases):
        for copy in out_copies(p):
            copy.wait()
        y_copy(p, z).wait_send()
        for_next(lambda up: z_copy(p, z, up), finish)
        for_next(lambda up: side_copy(p, z, up), finish)
        for side in range(2):
            core_copy(p, z, side).wait_send()
        for distance in range(1, nz):
            finish_plane(p, distance)
            core_copy(p, plane_at(distance), 1).wait_send()


def fused_body(nblk, nh, queries, key_rows, value_rows, visit_ids, span_order):
    rows = queries.shape[0]
    block = rows * nh
    phases = KV_HEADS // nh
    nz = nblk // 4
    dma = pltpu.SemaphoreType.DMA
    any_spec = pl.BlockSpec(memory_space=pl.ANY)
    return pl.pallas_call(
        functools.partial(fused_kernel, (nz, nh, rows, phases)),
        out_shape=jax.ShapeDtypeStruct(queries.shape, jnp.bfloat16),
        in_specs=[
            any_spec,
            any_spec,
            any_spec,
            pl.BlockSpec(memory_space=pltpu.VMEM),
            pl.BlockSpec(memory_space=pltpu.SMEM),
        ],
        out_specs=any_spec,
        scratch_shapes=[
            pltpu.VMEM((phases, 2, nblk * block, HEAD_DIM), jnp.bfloat16),
            pltpu.VMEM((phases, nh, rows, GROUP * HEAD_DIM), jnp.bfloat16),
            pltpu.VMEM((phases, nh, rows, GROUP * HEAD_DIM), jnp.bfloat16),
            pltpu.VMEM((nblk * block, GROUP * block), jnp.float32),
            dma((phases, nblk)),
            dma((phases, nz)),
            dma((phases, nz)),
            dma((phases, 2, nz)),
            dma((phases, 2, nz)),
            dma((phases, 2, nz)),
            dma((phases, nh - 1, 3)),
            dma((phases, nh - 1, 3)),
            dma((phases, 3)),
            dma((phases, nh - 1)),
            dma((phases, nh - 1)),
            dma((phases,)),
        ],
        compiler_params=pltpu.CompilerParams(
            collective_id=0, has_side_effects=True, vmem_limit_bytes=60 * 2**20
        ),
        name="visit_attention",
    )(queries, key_rows, value_rows, visit_ids.reshape(-1, 128), span_order)


def solution(mesh):
    placed = (
        P(("blk", "head"), None),
        P(("blk", "head"), None),
        P(("blk", "head"), None),
        P(),
        P(),
    )
    nblk, nh = mesh.shape["blk"], mesh.shape["head"]

    def body(queries, *rest):
        if queries.shape[0] % 16 == 0 and nblk % 4 == 0 and KV_HEADS % nh == 0:
            return fused_body(nblk, nh, queries, *rest)
        return gathered_body(queries, *rest)

    return jax.shard_map(
        body, mesh=mesh, in_specs=placed, out_specs=P(("blk", "head"), None), check_vma=False
    )
```

```python
import functools

import jax
import jax.numpy as jnp
from jax import lax
from jax.experimental import pallas as pl
from jax.experimental.pallas import tpu as pltpu
from jax.sharding import PartitionSpec as P

HEADS = 32
KV_HEADS = 8
HEAD_DIM = 128
VISITS = 4
GROUP = HEADS // KV_HEADS
LOG2E = 1.4426950408889634

MESH = pl.DeviceIdType.MESH

masked_score = -1e30


def span_of(cycle_positions, span_order):
    table_index = jnp.arange(span_order.shape[0], dtype=jnp.int32)
    picked = jnp.where(cycle_positions[:, None] == table_index[None, :], span_order[None, :], 0)
    return jnp.sum(picked, axis=1)


def gathered_body(queries, key_rows, value_rows, visit_ids, span_order):
    head_queries, head_keys, head_values = (
        lax.all_to_all(queries, "head", split_axis=1, concat_axis=0, tiled=True),
        lax.all_to_all(key_rows, "head", split_axis=1, concat_axis=0, tiled=True),
        lax.all_to_all(value_rows, "head", split_axis=1, concat_axis=0, tiled=True),
    )
    row_count = head_queries.shape[0]
    group_size = HEADS // KV_HEADS
    local_heads = head_keys.shape[1] // HEAD_DIM
    grouped = head_queries.reshape(row_count, local_heads, group_size, HEAD_DIM)
    cycle_index = lax.axis_index("blk")
    score_scale = HEAD_DIM ** (-0.5)
    my_span = span_of(jnp.full((1,), cycle_index, jnp.int32), span_order)[0]
    query_pos = my_span * row_count + jnp.arange(row_count, dtype=jnp.int32)
    query_visit = jnp.take(visit_ids, query_pos)

    def attend(state_now, kv_block, first_row):
        width = kv_block.shape[1]
        global_rows = first_row + jnp.arange(width, dtype=jnp.int32)
        key_pos = (
            span_of(global_rows // row_count, span_order) * row_count + global_rows % row_count
        )
        key_visit = jnp.take(visit_ids, key_pos)
        allowed = (key_pos[None, :] <= query_pos[:, None]) & (
            key_visit[None, :] == query_visit[:, None]
        )
        run_max, run_total, run_acc = state_now
        key_heads = kv_block[0].reshape(width, local_heads, HEAD_DIM)
        value_heads = kv_block[1].reshape(width, local_heads, HEAD_DIM)
        scores = (
            jnp.einsum("qhgd,khd->qhgk", grouped, key_heads, preferred_element_type=jnp.float32)
            * score_scale
        )
        mask_wide = allowed[:, None, None, :]
        masked = jnp.where(mask_wide, scores, masked_score)
        new_max = jnp.maximum(run_max, jnp.max(masked, axis=-1))
        factor = jnp.exp(run_max - new_max)
        weights = jnp.where(mask_wide, jnp.exp(masked - new_max[..., None]), 0.0)
        new_total = run_total * factor + jnp.sum(weights, axis=-1)
        new_acc = run_acc * factor[..., None] + jnp.einsum(
            "qhgk,khd->qhgd",
            weights.astype(jnp.bfloat16),
            value_heads,
            preferred_element_type=jnp.float32,
        )
        return (new_max, new_total, new_acc)

    kv_local = jnp.stack([head_keys, head_values])
    stat_shape = (row_count, local_heads, group_size)
    initial = (
        jnp.full(stat_shape, masked_score, jnp.float32),
        jnp.zeros(stat_shape, jnp.float32),
        jnp.zeros(stat_shape + (HEAD_DIM,), jnp.float32),
    )
    part_rows = lax.all_gather(kv_local, "blk", axis=1, tiled=True)
    width = part_rows.shape[1]
    step_rows = width
    step_rows = 4 * row_count

    def inner(turn_index, state_in):
        offset = turn_index * step_rows
        sub_block = lax.dynamic_slice_in_dim(part_rows, offset, step_rows, 1)
        return attend(state_in, sub_block, offset)

    state_now = lax.fori_loop(0, width // step_rows, inner, initial)
    run_max, run_total, run_acc = state_now
    attended_local = (run_acc / run_total[..., None]).astype(jnp.bfloat16)
    attended_local = attended_local.reshape(row_count, local_heads * group_size * HEAD_DIM)
    return lax.all_to_all(attended_local, "head", split_axis=0, concat_axis=1, tiled=True)


def fused_kernel(
    dims, q_ref, k_ref, v_ref, visit_ref, span_ref, out_ref,
    kv, qs, outs, bias,
    kv_recv, side_recv, y_send, core_send, z_send, side_send, x_send, x_recv, own_sem, out_send, out_recv, out_own,
):
    nz, nh, rows, phases = dims
    nblk = 4 * nz
    block = nh * rows
    keys = nblk * block
    me = lax.axis_index("blk")
    x = lax.axis_index("head")
    z, y, core = me // 4, (me // 2) % 2, me % 2

    def index_of(z_at, y_at, core_at):
        return z_at * 4 + y_at * 2 + core_at

    y_id = index_of(z, 1 - y, core)
    core_id = index_of(z, y, 1 - core)
    x_peers = [lax.rem(x + step, nh) for step in range(1, nh)]
    side_rows = max(16, block // (2 * (nz - 1)) // 16 * 16)

    def next_plane(up):
        return z + 1 if up else z - 1

    def has_next(up):
        return z + 1 < nz if up else z > 0

    barrier = pltpu.get_barrier_semaphore()
    for blk in (y_id, core_id):
        pl.semaphore_signal(barrier, inc=1, device_id=(blk, x), device_id_type=MESH)
    for xp in x_peers:
        pl.semaphore_signal(barrier, inc=1, device_id=(me, xp), device_id_type=MESH)
    for up in (True, False):

        @pl.when(has_next(up))
        def _(up=up):
            target = index_of(next_plane(up), y, core)
            pl.semaphore_signal(barrier, inc=1, device_id=(target, x), device_id_type=MESH)

    def sources(p, to):
        kv_at = pl.multiple_of((to * phases + p) * HEAD_DIM, HEAD_DIM)
        q_at = pl.multiple_of((to * phases + p) * GROUP * HEAD_DIM, GROUP * HEAD_DIM)
        return (
            k_ref.at[:, pl.ds(kv_at, HEAD_DIM)],
            v_ref.at[:, pl.ds(kv_at, HEAD_DIM)],
            q_ref.at[:, pl.ds(q_at, GROUP * HEAD_DIM)],
        )

    def landing(p, source):
        row = pl.multiple_of(me * block + source * rows, 16)
        return (
            kv.at[p, 0, pl.ds(row, rows), :],
            kv.at[p, 1, pl.ds(row, rows), :],
            qs.at[p, source],
        )

    def own_copies(p, kinds=3, first_kind=0):
        pairs = list(zip(sources(p, x), landing(p, x)))
        return [
            pltpu.make_async_copy(*pairs[kind], own_sem.at[p, kind])
            for kind in range(first_kind, kinds)
        ]

    def x_copies(p, kinds):
        result = []
        for step, xp in enumerate(x_peers):
            from_refs, to_refs = sources(p, xp), landing(p, x)
            for kind in kinds:
                result.append(
                    pltpu.make_async_remote_copy(
                        src_ref=from_refs[kind], dst_ref=to_refs[kind],
                        send_sem=x_send.at[p, step, kind], recv_sem=x_recv.at[p, step, kind],
                        device_id=(me, xp), device_id_type=MESH,
                    )
                )
        return result

    def rows_ref(p, blk, first_row, count):
        at = pl.multiple_of(blk * block + first_row, 16)
        return kv.at[p, :, pl.ds(at, count), :]

    def remote(ref, send_sem, recv_sem, target):
        return pltpu.make_async_remote_copy(
            src_ref=ref, dst_ref=ref, send_sem=send_sem, recv_sem=recv_sem,
            device_id=(target, x), device_id_type=MESH,
        )

    def whole_copy(p, blk, send_sem, target):
        return remote(rows_ref(p, blk, 0, block), send_sem, kv_recv.at[p, blk], target)

    def y_copy(p, plane):
        blk = index_of(plane, y, core)
        if plane is z:
            return whole_copy(p, blk, y_send.at[p, plane], y_id)
        ref = rows_ref(p, blk, side_rows, block - side_rows)
        return remote(ref, y_send.at[p, plane], kv_recv.at[p, blk], y_id)

    def core_copy(p, plane, side):
        blk = index_of(plane, y if side == 0 else 1 - y, core)
        return whole_copy(p, blk, core_send.at[p, side, plane], core_id)

    def z_copy(p, plane, up):
        blk, to = index_of(plane, y, core), index_of(next_plane(up), y, core)
        return whole_copy(p, blk, z_send.at[p, int(up), plane], to)

    def side_copy(p, plane, up):
        blk, to = index_of(plane, 1 - y, core), index_of(next_plane(up), y, core)
        ref = rows_ref(p, blk, 0, side_rows)
        return remote(ref, side_send.at[p, int(up), plane], side_recv.at[p, plane], to)

    def await_whole(p, blk):
        whole_copy(p, blk, y_send.at[p, 0], y_id).wait_recv()

    def for_next(make, act):
        for up in (True, False):
            pl.when(has_next(up))(functools.partial(lambda up: act(make(up)), up))

    def start(copy):
        copy.start()

    def finish(copy):
        copy.wait_send()

    def start_own(p):
        for copy in own_copies(p, 2):
            copy.wait()
        for copy in x_copies(p, (0, 1)):
            copy.wait()
        y_copy(p, z).start()
        for_next(lambda up: z_copy(p, z, up), start)
        core_copy(p, z, 0).start()

    def pass_peer(p):
        await_whole(p, index_of(z, 1 - y, core))
        for_next(lambda up: side_copy(p, z, up), start)
        core_copy(p, z, 1).start()

    def from_planes(distance, act):
        for up in (True, False):
            plane = z - distance if up else z + distance
            exists = plane >= 0 if up else plane < nz
            pl.when(exists)(functools.partial(act, plane, up))

    def pass_plane(p, distance):
        def act(plane, up):
            await_whole(p, index_of(plane, y, core))

            @pl.when(has_next(up))
            def _():
                z_copy(p, plane, up).start()

            y_copy(p, plane).start()
            core_copy(p, plane, 0).start()
            remote(
                rows_ref(p, index_of(plane, 1 - y, core), 0, side_rows),
                side_send.at[p, 0, 0], side_recv.at[p, plane], y_id,
            ).wait_recv()

            @pl.when(has_next(up))
            def _():
                side_copy(p, plane, up).start()

        from_planes(distance, act)

    def finish_plane(p, distance):
        def act(plane, up):
            @pl.when(has_next(up))
            def _():
                z_copy(p, plane, up).wait_send()
                side_copy(p, plane, up).wait_send()

            y_copy(p, plane).wait_send()
            core_copy(p, plane, 0).wait_send()

        from_planes(distance, act)

    def plane_at(rank):
        return lax.rem(z + jnp.where(2 * z < nz, rank, nz - rank), nz)

    def pass_far(p, rank):
        plane = plane_at(rank)
        blk = index_of(plane, 1 - y, core)
        remote(
            rows_ref(p, blk, side_rows, block - side_rows),
            y_send.at[p, 0], kv_recv.at[p, blk], y_id,
        ).wait_recv()
        core_copy(p, plane, 1).start()

    for p in range(phases):
        for copy in own_copies(p):
            copy.start()

    columns = GROUP * block
    column = lax.broadcasted_iota(jnp.int32, (1, columns), 1)
    offset = column
    for g in range(1, GROUP):
        offset = jnp.where(column >= g * block, column - g * block, offset)
    query_pos = span_ref[me] * block + offset
    first = jnp.zeros((1, columns), jnp.int32)
    visits = visit_ref[...]
    for visit in range(1, VISITS):
        begin = jnp.sum(jnp.where(visits < visit, 1.0, 0.0), axis=1, keepdims=True)
        begin = jnp.sum(begin, axis=0, keepdims=True).astype(jnp.int32)
        first = jnp.where(begin <= query_pos, jnp.maximum(first, begin), first)
    row = lax.broadcasted_iota(jnp.int32, (block, 1), 0)

    def mask_block(blk, carry):
        key_pos = span_ref[blk] * block + row
        allowed = (key_pos <= query_pos) & (key_pos >= first)
        bias[pl.ds(pl.multiple_of(blk * block, 16), block), :] = jnp.where(allowed, 0.0, -jnp.inf)
        return carry

    lax.fori_loop(0, nblk, mask_block, 0)

    planes_beside = jnp.minimum(z, 1) + jnp.minimum(nz - 1 - z, 1)
    pl.semaphore_wait(barrier, 1 + nh + planes_beside)

    def start_x(p, kinds):
        for copy in x_copies(p, kinds):
            copy.start()

    chunk = 2 * block
    batch = GROUP
    scale = HEAD_DIM**-0.5 * LOG2E
    lowest = -3.0e38

    def compute(p, events):
        at = 0
        query = jnp.concatenate(
            [
                jnp.concatenate([qs[p, h, :, g * HEAD_DIM : (g + 1) * HEAD_DIM] for h in range(nh)], axis=0)
                for g in range(at, at + batch)
            ],
            axis=0,
        )

        query_t = jnp.transpose(query)

        def step(index, state):
            for slot, event in events:
                pl.when(index == slot)(event)
            run_max, run_acc = state
            starts = []
            for rank in (2 * index, 2 * index + 1):
                plane = plane_at(lax.rem(rank, nz))
                chip = plane * 2 + jnp.where(rank < nz, y, 1 - y)
                await_whole(p, chip * 2 + 1 - core)
                starts.append(pl.multiple_of(chip * chunk, 128))
            key = jnp.concatenate([kv[p, 0, pl.ds(at, chunk), :] for at in starts], axis=0)
            value = jnp.concatenate([kv[p, 1, pl.ds(at, chunk), :] for at in starts], axis=0)
            mask = jnp.concatenate([bias[pl.ds(at, chunk), :] for at in starts], axis=0)
            extended = jnp.concatenate(
                [jnp.transpose(value), jnp.ones((16, 2 * chunk), jnp.bfloat16)], axis=0
            )
            score = jnp.dot(key, query_t, preferred_element_type=jnp.float32)
            shifted = score * scale + mask
            new_max = jnp.maximum(run_max, jnp.max(shifted, axis=0, keepdims=True))
            weight = jnp.exp2(shifted - new_max).astype(jnp.bfloat16)
            factor = jnp.exp2(run_max - new_max)
            new_acc = run_acc * factor + jnp.dot(
                extended, weight, preferred_element_type=jnp.float32
            )
            return new_max, new_acc

        initial = (
            jnp.full((1, columns), lowest, jnp.float32),
            jnp.zeros((HEAD_DIM + 16, columns), jnp.float32),
        )
        _, acc = lax.fori_loop(0, nz, step, initial)
        result = jnp.transpose(acc[:HEAD_DIM] / acc[HEAD_DIM : HEAD_DIM + 1]).astype(jnp.bfloat16)
        for i in range(batch):
            for h in range(nh):
                first_row = i * block + h * rows
                outs[p, h, :, (at + i) * HEAD_DIM : (at + i + 1) * HEAD_DIM] = result[
                    first_row : first_row + rows
                ]

    width = GROUP * HEAD_DIM

    def out_copies(p):
        place = out_ref.at[:, pl.ds(pl.multiple_of((x * phases + p) * width, width), width)]
        copies = [pltpu.make_async_copy(outs.at[p, x], place, out_own.at[p])]
        for step, xp in enumerate(x_peers):
            copies.append(
                pltpu.make_async_remote_copy(
                    src_ref=outs.at[p, xp], dst_ref=place,
                    send_sem=out_send.at[p, step], recv_sem=out_recv.at[p, step],
                    device_id=(me, xp), device_id_type=MESH,
                )
            )
        return copies

    def events_of(p):
        events = []
        for rank in range(1, nz):
            events.append((min(rank, nz - 2), functools.partial(pass_far, p, rank)))
        if p + 1 < phases:
            events.append((0, functools.partial(pass_peer, p + 1)))
            for distance in range(1, nz):
                events.append((distance, functools.partial(pass_plane, p + 1, distance)))
        return events

    start_x(0, (0, 1))
    start_own(0)
    for p in range(1, min(2, phases)):
        start_x(p, (0, 1))
        start_x(p - 1, (2,))
        start_own(p)
    pass_peer(0)
    for p in range(min(2, phases), min(3, phases)):
        start_x(p, (0, 1))
    start_x(min(2, phases) - 1, (2,))
    for distance in range(1, nz):
        pass_plane(0, distance)
    for p in range(phases):
        if p + 2 < phases:
            start_own(p + 2)
            start_x(p + 2, (2,))
            if p + 3 < phases:
                start_x(p + 3, (0, 1))
        for copy in own_copies(p, 3, 2):
            copy.wait()
        for copy in x_copies(p, (2,)):
            copy.wait()
        compute(p, events_of(p))
        for copy in out_copies(p):
            copy.start()
    for p in range(phases):
        for copy in out_copies(p):
            copy.wait()
        y_copy(p, z).wait_send()
        for_next(lambda up: z_copy(p, z, up), finish)
        for_next(lambda up: side_copy(p, z, up), finish)
        for side in range(2):
            core_copy(p, z, side).wait_send()
        for distance in range(1, nz):
            finish_plane(p, distance)
            core_copy(p, plane_at(distance), 1).wait_send()


def fused_body(nblk, nh, queries, key_rows, value_rows, visit_ids, span_order):
    rows = queries.shape[0]
    block = rows * nh
    phases = KV_HEADS // nh
    nz = nblk // 4
    dma = pltpu.SemaphoreType.DMA
    any_spec = pl.BlockSpec(memory_space=pl.ANY)
    return pl.pallas_call(
        functools.partial(fused_kernel, (nz, nh, rows, phases)),
        out_shape=jax.ShapeDtypeStruct(queries.shape, jnp.bfloat16),
        in_specs=[
            any_spec,
            any_spec,
            any_spec,
            pl.BlockSpec(memory_space=pltpu.VMEM),
            pl.BlockSpec(memory_space=pltpu.SMEM),
        ],
        out_specs=any_spec,
        scratch_shapes=[
            pltpu.VMEM((phases, 2, nblk * block, HEAD_DIM), jnp.bfloat16),
            pltpu.VMEM((phases, nh, rows, GROUP * HEAD_DIM), jnp.bfloat16),
            pltpu.VMEM((phases, nh, rows, GROUP * HEAD_DIM), jnp.bfloat16),
            pltpu.VMEM((nblk * block, GROUP * block), jnp.float32),
            dma((phases, nblk)),
            dma((phases, nz)),
            dma((phases, nz)),
            dma((phases, 2, nz)),
            dma((phases, 2, nz)),
            dma((phases, 2, nz)),
            dma((phases, nh - 1, 3)),
            dma((phases, nh - 1, 3)),
            dma((phases, 3)),
            dma((phases, nh - 1)),
            dma((phases, nh - 1)),
            dma((phases,)),
        ],
        compiler_params=pltpu.CompilerParams(
            collective_id=0, has_side_effects=True, vmem_limit_bytes=60 * 2**20
        ),
        name="visit_attention",
    )(queries, key_rows, value_rows, visit_ids.reshape(-1, 128), span_order)


def solution(mesh):
    placed = (
        P(("blk", "head"), None),
        P(("blk", "head"), None),
        P(("blk", "head"), None),
        P(),
        P(),
    )
    nblk, nh = mesh.shape["blk"], mesh.shape["head"]

    def body(queries, *rest):
        if queries.shape[0] % 16 == 0 and nblk % 8 == 0 and KV_HEADS % nh == 0:
            return fused_body(nblk, nh, queries, *rest)
        return gathered_body(queries, *rest)

    return jax.shard_map(
        body, mesh=mesh, in_specs=placed, out_specs=P(("blk", "head"), None), check_vma=False
    )
```

```python
import functools

import jax
import jax.numpy as jnp
from jax import lax
from jax.experimental import pallas as pl
from jax.experimental.pallas import tpu as pltpu
from jax.sharding import PartitionSpec as P

HEADS = 32
KV_HEADS = 8
HEAD_DIM = 128
VISITS = 4
GROUP = HEADS // KV_HEADS
LOG2E = 1.4426950408889634

MESH = pl.DeviceIdType.MESH

masked_score = -1e30


def span_of(cycle_positions, span_order):
    table_index = jnp.arange(span_order.shape[0], dtype=jnp.int32)
    picked = jnp.where(cycle_positions[:, None] == table_index[None, :], span_order[None, :], 0)
    return jnp.sum(picked, axis=1)


def gathered_body(queries, key_rows, value_rows, visit_ids, span_order):
    head_queries, head_keys, head_values = (
        lax.all_to_all(queries, "head", split_axis=1, concat_axis=0, tiled=True),
        lax.all_to_all(key_rows, "head", split_axis=1, concat_axis=0, tiled=True),
        lax.all_to_all(value_rows, "head", split_axis=1, concat_axis=0, tiled=True),
    )
    row_count = head_queries.shape[0]
    group_size = HEADS // KV_HEADS
    local_heads = head_keys.shape[1] // HEAD_DIM
    grouped = head_queries.reshape(row_count, local_heads, group_size, HEAD_DIM)
    cycle_index = lax.axis_index("blk")
    score_scale = HEAD_DIM ** (-0.5)
    my_span = span_of(jnp.full((1,), cycle_index, jnp.int32), span_order)[0]
    query_pos = my_span * row_count + jnp.arange(row_count, dtype=jnp.int32)
    query_visit = jnp.take(visit_ids, query_pos)

    def attend(state_now, kv_block, first_row):
        width = kv_block.shape[1]
        global_rows = first_row + jnp.arange(width, dtype=jnp.int32)
        key_pos = (
            span_of(global_rows // row_count, span_order) * row_count + global_rows % row_count
        )
        key_visit = jnp.take(visit_ids, key_pos)
        allowed = (key_pos[None, :] <= query_pos[:, None]) & (
            key_visit[None, :] == query_visit[:, None]
        )
        run_max, run_total, run_acc = state_now
        key_heads = kv_block[0].reshape(width, local_heads, HEAD_DIM)
        value_heads = kv_block[1].reshape(width, local_heads, HEAD_DIM)
        scores = (
            jnp.einsum("qhgd,khd->qhgk", grouped, key_heads, preferred_element_type=jnp.float32)
            * score_scale
        )
        mask_wide = allowed[:, None, None, :]
        masked = jnp.where(mask_wide, scores, masked_score)
        new_max = jnp.maximum(run_max, jnp.max(masked, axis=-1))
        factor = jnp.exp(run_max - new_max)
        weights = jnp.where(mask_wide, jnp.exp(masked - new_max[..., None]), 0.0)
        new_total = run_total * factor + jnp.sum(weights, axis=-1)
        new_acc = run_acc * factor[..., None] + jnp.einsum(
            "qhgk,khd->qhgd",
            weights.astype(jnp.bfloat16),
            value_heads,
            preferred_element_type=jnp.float32,
        )
        return (new_max, new_total, new_acc)

    kv_local = jnp.stack([head_keys, head_values])
    stat_shape = (row_count, local_heads, group_size)
    initial = (
        jnp.full(stat_shape, masked_score, jnp.float32),
        jnp.zeros(stat_shape, jnp.float32),
        jnp.zeros(stat_shape + (HEAD_DIM,), jnp.float32),
    )
    part_rows = lax.all_gather(kv_local, "blk", axis=1, tiled=True)
    width = part_rows.shape[1]
    step_rows = width
    step_rows = 4 * row_count

    def inner(turn_index, state_in):
        offset = turn_index * step_rows
        sub_block = lax.dynamic_slice_in_dim(part_rows, offset, step_rows, 1)
        return attend(state_in, sub_block, offset)

    state_now = lax.fori_loop(0, width // step_rows, inner, initial)
    run_max, run_total, run_acc = state_now
    attended_local = (run_acc / run_total[..., None]).astype(jnp.bfloat16)
    attended_local = attended_local.reshape(row_count, local_heads * group_size * HEAD_DIM)
    return lax.all_to_all(attended_local, "head", split_axis=0, concat_axis=1, tiled=True)


def fused_kernel(
    dims, q_ref, k_ref, v_ref, visit_ref, span_ref, out_ref,
    kv, qs, outs, bias,
    kv_recv, side_recv, y_send, core_send, z_send, side_send, x_send, x_recv, own_sem, out_send, out_recv, out_own,
):
    nz, nh, rows, phases = dims
    nblk = 4 * nz
    block = nh * rows
    keys = nblk * block
    me = lax.axis_index("blk")
    x = lax.axis_index("head")
    z, y, core = me // 4, (me // 2) % 2, me % 2

    def index_of(z_at, y_at, core_at):
        return z_at * 4 + y_at * 2 + core_at

    y_id = index_of(z, 1 - y, core)
    core_id = index_of(z, y, 1 - core)
    x_peers = [lax.rem(x + step, nh) for step in range(1, nh)]
    side_rows = max(16, block // (2 * (nz - 1)) // 16 * 16)

    def next_plane(up):
        return z + 1 if up else z - 1

    def has_next(up):
        return z + 1 < nz if up else z > 0

    barrier = pltpu.get_barrier_semaphore()
    for blk in (y_id, core_id):
        pl.semaphore_signal(barrier, inc=1, device_id=(blk, x), device_id_type=MESH)
    for xp in x_peers:
        pl.semaphore_signal(barrier, inc=1, device_id=(me, xp), device_id_type=MESH)
    for up in (True, False):

        @pl.when(has_next(up))
        def _(up=up):
            target = index_of(next_plane(up), y, core)
            pl.semaphore_signal(barrier, inc=1, device_id=(target, x), device_id_type=MESH)

    def sources(p, to):
        kv_at = pl.multiple_of((to * phases + p) * HEAD_DIM, HEAD_DIM)
        q_at = pl.multiple_of((to * phases + p) * GROUP * HEAD_DIM, GROUP * HEAD_DIM)
        return (
            k_ref.at[:, pl.ds(kv_at, HEAD_DIM)],
            v_ref.at[:, pl.ds(kv_at, HEAD_DIM)],
            q_ref.at[:, pl.ds(q_at, GROUP * HEAD_DIM)],
        )

    def landing(p, source):
        row = pl.multiple_of(me * block + source * rows, 16)
        return (
            kv.at[p, 0, pl.ds(row, rows), :],
            kv.at[p, 1, pl.ds(row, rows), :],
            qs.at[p, source],
        )

    def own_copies(p, kinds=3, first_kind=0):
        pairs = list(zip(sources(p, x), landing(p, x)))
        return [
            pltpu.make_async_copy(*pairs[kind], own_sem.at[p, kind])
            for kind in range(first_kind, kinds)
        ]

    def x_copies(p, kinds):
        result = []
        for step, xp in enumerate(x_peers):
            from_refs, to_refs = sources(p, xp), landing(p, x)
            for kind in kinds:
                result.append(
                    pltpu.make_async_remote_copy(
                        src_ref=from_refs[kind], dst_ref=to_refs[kind],
                        send_sem=x_send.at[p, step, kind], recv_sem=x_recv.at[p, step, kind],
                        device_id=(me, xp), device_id_type=MESH,
                    )
                )
        return result

    def rows_ref(p, blk, first_row, count):
        at = pl.multiple_of(blk * block + first_row, 16)
        return kv.at[p, :, pl.ds(at, count), :]

    def remote(ref, send_sem, recv_sem, target):
        return pltpu.make_async_remote_copy(
            src_ref=ref, dst_ref=ref, send_sem=send_sem, recv_sem=recv_sem,
            device_id=(target, x), device_id_type=MESH,
        )

    def whole_copy(p, blk, send_sem, target):
        return remote(rows_ref(p, blk, 0, block), send_sem, kv_recv.at[p, blk], target)

    def y_copy(p, plane):
        blk = index_of(plane, y, core)
        if plane is z:
            return whole_copy(p, blk, y_send.at[p, plane], y_id)
        ref = rows_ref(p, blk, side_rows, block - side_rows)
        return remote(ref, y_send.at[p, plane], kv_recv.at[p, blk], y_id)

    def core_copy(p, plane, side):
        blk = index_of(plane, y if side == 0 else 1 - y, core)
        return whole_copy(p, blk, core_send.at[p, side, plane], core_id)

    def z_copy(p, plane, up):
        blk, to = index_of(plane, y, core), index_of(next_plane(up), y, core)
        return whole_copy(p, blk, z_send.at[p, int(up), plane], to)

    def side_copy(p, plane, up):
        blk, to = index_of(plane, 1 - y, core), index_of(next_plane(up), y, core)
        ref = rows_ref(p, blk, 0, side_rows)
        return remote(ref, side_send.at[p, int(up), plane], side_recv.at[p, plane], to)

    def await_whole(p, blk):
        whole_copy(p, blk, y_send.at[p, 0], y_id).wait_recv()

    def for_next(make, act):
        for up in (True, False):
            pl.when(has_next(up))(functools.partial(lambda up: act(make(up)), up))

    def start(copy):
        copy.start()

    def finish(copy):
        copy.wait_send()

    def start_own(p):
        for copy in own_copies(p, 2):
            copy.wait()
        for copy in x_copies(p, (0, 1)):
            copy.wait()
        y_copy(p, z).start()
        for_next(lambda up: z_copy(p, z, up), start)
        core_copy(p, z, 0).start()

    def pass_peer(p):
        await_whole(p, index_of(z, 1 - y, core))
        for_next(lambda up: side_copy(p, z, up), start)
        core_copy(p, z, 1).start()

    def from_planes(distance, act):
        for up in (True, False):
            plane = z - distance if up else z + distance
            exists = plane >= 0 if up else plane < nz
            pl.when(exists)(functools.partial(act, plane, up))

    def pass_plane(p, distance):
        def act(plane, up):
            await_whole(p, index_of(plane, y, core))

            @pl.when(has_next(up))
            def _():
                z_copy(p, plane, up).start()

            y_copy(p, plane).start()
            core_copy(p, plane, 0).start()
            remote(
                rows_ref(p, index_of(plane, 1 - y, core), 0, side_rows),
                side_send.at[p, 0, 0], side_recv.at[p, plane], y_id,
            ).wait_recv()

            @pl.when(has_next(up))
            def _():
                side_copy(p, plane, up).start()

        from_planes(distance, act)

    def finish_plane(p, distance):
        def act(plane, up):
            @pl.when(has_next(up))
            def _():
                z_copy(p, plane, up).wait_send()
                side_copy(p, plane, up).wait_send()

            y_copy(p, plane).wait_send()
            core_copy(p, plane, 0).wait_send()

        from_planes(distance, act)

    def plane_at(rank):
        return lax.rem(z + jnp.where(2 * z < nz, rank, nz - rank), nz)

    def pass_far(p, rank):
        plane = plane_at(rank)
        blk = index_of(plane, 1 - y, core)
        remote(
            rows_ref(p, blk, side_rows, block - side_rows),
            y_send.at[p, 0], kv_recv.at[p, blk], y_id,
        ).wait_recv()
        core_copy(p, plane, 1).start()

    for p in range(phases):
        for copy in own_copies(p):
            copy.start()

    columns = GROUP * block
    column = lax.broadcasted_iota(jnp.int32, (1, columns), 1)
    offset = column
    for g in range(1, GROUP):
        offset = jnp.where(column >= g * block, column - g * block, offset)
    query_pos = span_ref[me] * block + offset
    first = jnp.zeros((1, columns), jnp.int32)
    visits = visit_ref[...]
    for visit in range(1, VISITS):
        begin = jnp.sum(jnp.where(visits < visit, 1.0, 0.0), axis=1, keepdims=True)
        begin = jnp.sum(begin, axis=0, keepdims=True).astype(jnp.int32)
        first = jnp.where(begin <= query_pos, jnp.maximum(first, begin), first)
    row = lax.broadcasted_iota(jnp.int32, (block, 1), 0)

    def mask_block(blk, carry):
        key_pos = span_ref[blk] * block + row
        allowed = (key_pos <= query_pos) & (key_pos >= first)
        bias[pl.ds(pl.multiple_of(blk * block, 16), block), :] = jnp.where(allowed, 0.0, -jnp.inf)
        return carry

    planes_beside = jnp.minimum(z, 1) + jnp.minimum(nz - 1 - z, 1)
    pl.semaphore_wait(barrier, 1 + nh + planes_beside)

    def start_x(p, kinds):
        for copy in x_copies(p, kinds):
            copy.start()

    chunk = 2 * block
    batch = GROUP
    scale = HEAD_DIM**-0.5 * LOG2E
    lowest = -3.0e38

    def compute(p, events):
        at = 0
        query = jnp.concatenate(
            [
                jnp.concatenate([qs[p, h, :, g * HEAD_DIM : (g + 1) * HEAD_DIM] for h in range(nh)], axis=0)
                for g in range(at, at + batch)
            ],
            axis=0,
        )

        query_t = jnp.transpose(query)

        def step(index, state):
            for slot, event in events:
                pl.when(index == slot)(event)
            run_max, run_acc = state
            starts = []
            for rank in (2 * index, 2 * index + 1):
                plane = plane_at(lax.rem(rank, nz))
                chip = plane * 2 + jnp.where(rank < nz, y, 1 - y)
                await_whole(p, chip * 2 + 1 - core)
                starts.append(pl.multiple_of(chip * chunk, 128))
            key = jnp.concatenate([kv[p, 0, pl.ds(at, chunk), :] for at in starts], axis=0)
            value = jnp.concatenate([kv[p, 1, pl.ds(at, chunk), :] for at in starts], axis=0)
            mask = jnp.concatenate([bias[pl.ds(at, chunk), :] for at in starts], axis=0)
            extended = jnp.concatenate(
                [jnp.transpose(value), jnp.ones((16, 2 * chunk), jnp.bfloat16)], axis=0
            )
            score = jnp.dot(key, query_t, preferred_element_type=jnp.float32)
            shifted = score * scale + mask
            new_max = jnp.maximum(run_max, jnp.max(shifted, axis=0, keepdims=True))
            weight = jnp.exp2(shifted - new_max).astype(jnp.bfloat16)
            factor = jnp.exp2(run_max - new_max)
            new_acc = run_acc * factor + jnp.dot(
                extended, weight, preferred_element_type=jnp.float32
            )
            return new_max, new_acc

        initial = (
            jnp.full((1, columns), lowest, jnp.float32),
            jnp.zeros((HEAD_DIM + 16, columns), jnp.float32),
        )
        _, acc = lax.fori_loop(0, nz, step, initial)
        result = jnp.transpose(acc[:HEAD_DIM] / acc[HEAD_DIM : HEAD_DIM + 1]).astype(jnp.bfloat16)
        for i in range(batch):
            for h in range(nh):
                first_row = i * block + h * rows
                outs[p, h, :, (at + i) * HEAD_DIM : (at + i + 1) * HEAD_DIM] = result[
                    first_row : first_row + rows
                ]

    width = GROUP * HEAD_DIM

    def out_copies(p):
        place = out_ref.at[:, pl.ds(pl.multiple_of((x * phases + p) * width, width), width)]
        copies = [pltpu.make_async_copy(outs.at[p, x], place, out_own.at[p])]
        for step, xp in enumerate(x_peers):
            copies.append(
                pltpu.make_async_remote_copy(
                    src_ref=outs.at[p, xp], dst_ref=place,
                    send_sem=out_send.at[p, step], recv_sem=out_recv.at[p, step],
                    device_id=(me, xp), device_id_type=MESH,
                )
            )
        return copies

    def events_of(p):
        events = []
        if p == 0:
            events.append((nz // 2 - 1, functools.partial(pass_plane, 0, nz - 1)))
        for rank in range(1, nz):
            events.append((min(rank, nz - 2), functools.partial(pass_far, p, rank)))
        if p + 1 < phases:
            events.append((0, functools.partial(pass_peer, p + 1)))
            for distance in range(1, nz):
                events.append((distance, functools.partial(pass_plane, p + 1, distance)))
        return events

    start_x(0, (0, 1))
    lax.fori_loop(0, nblk, mask_block, 0)
    start_own(0)
    if phases > 1:
        start_x(1, (0, 1))
    start_x(0, (2,))
    pass_peer(0)
    for distance in range(1, nz - 1):
        pass_plane(0, distance)
    if phases > 1:
        start_own(1)
        start_x(1, (2,))
    if phases > 2:
        start_x(2, (0, 1))
    for p in range(phases):
        if p + 2 < phases:
            start_own(p + 2)
            start_x(p + 2, (2,))
            if p + 3 < phases:
                start_x(p + 3, (0, 1))
        for copy in own_copies(p, 3, 2):
            copy.wait()
        for copy in x_copies(p, (2,)):
            copy.wait()
        compute(p, events_of(p))
        for copy in out_copies(p):
            copy.start()
    for p in range(phases):
        for copy in out_copies(p):
            copy.wait()
        y_copy(p, z).wait_send()
        for_next(lambda up: z_copy(p, z, up), finish)
        for_next(lambda up: side_copy(p, z, up), finish)
        for side in range(2):
            core_copy(p, z, side).wait_send()
        for distance in range(1, nz):
            finish_plane(p, distance)
            core_copy(p, plane_at(distance), 1).wait_send()


def fused_body(nblk, nh, queries, key_rows, value_rows, visit_ids, span_order):
    rows = queries.shape[0]
    block = rows * nh
    phases = KV_HEADS // nh
    nz = nblk // 4
    dma = pltpu.SemaphoreType.DMA
    any_spec = pl.BlockSpec(memory_space=pl.ANY)
    return pl.pallas_call(
        functools.partial(fused_kernel, (nz, nh, rows, phases)),
        out_shape=jax.ShapeDtypeStruct(queries.shape, jnp.bfloat16),
        in_specs=[
            any_spec,
            any_spec,
            any_spec,
            pl.BlockSpec(memory_space=pltpu.VMEM),
            pl.BlockSpec(memory_space=pltpu.SMEM),
        ],
        out_specs=any_spec,
        scratch_shapes=[
            pltpu.VMEM((phases, 2, nblk * block, HEAD_DIM), jnp.bfloat16),
            pltpu.VMEM((phases, nh, rows, GROUP * HEAD_DIM), jnp.bfloat16),
            pltpu.VMEM((phases, nh, rows, GROUP * HEAD_DIM), jnp.bfloat16),
            pltpu.VMEM((nblk * block, GROUP * block), jnp.float32),
            dma((phases, nblk)),
            dma((phases, nz)),
            dma((phases, nz)),
            dma((phases, 2, nz)),
            dma((phases, 2, nz)),
            dma((phases, 2, nz)),
            dma((phases, nh - 1, 3)),
            dma((phases, nh - 1, 3)),
            dma((phases, 3)),
            dma((phases, nh - 1)),
            dma((phases, nh - 1)),
            dma((phases,)),
        ],
        compiler_params=pltpu.CompilerParams(
            collective_id=0, has_side_effects=True, vmem_limit_bytes=60 * 2**20
        ),
        name="visit_attention",
    )(queries, key_rows, value_rows, visit_ids.reshape(-1, 128), span_order)


def solution(mesh):
    placed = (
        P(("blk", "head"), None),
        P(("blk", "head"), None),
        P(("blk", "head"), None),
        P(),
        P(),
    )
    nblk, nh = mesh.shape["blk"], mesh.shape["head"]

    def body(queries, *rest):
        if queries.shape[0] % 16 == 0 and nblk % 8 == 0 and KV_HEADS % nh == 0:
            return fused_body(nblk, nh, queries, *rest)
        return gathered_body(queries, *rest)

    return jax.shard_map(
        body, mesh=mesh, in_specs=placed, out_specs=P(("blk", "head"), None), check_vma=False
    )
```

```python
import functools

import jax
import jax.numpy as jnp
from jax import lax
from jax.experimental import pallas as pl
from jax.experimental.pallas import tpu as pltpu
from jax.sharding import PartitionSpec as P

HEADS = 32
KV_HEADS = 8
HEAD_DIM = 128
VISITS = 4
GROUP = HEADS // KV_HEADS
LOG2E = 1.4426950408889634

MESH = pl.DeviceIdType.MESH

masked_score = -1e30


def span_of(cycle_positions, span_order):
    table_index = jnp.arange(span_order.shape[0], dtype=jnp.int32)
    picked = jnp.where(cycle_positions[:, None] == table_index[None, :], span_order[None, :], 0)
    return jnp.sum(picked, axis=1)


def gathered_body(queries, key_rows, value_rows, visit_ids, span_order):
    head_queries, head_keys, head_values = (
        lax.all_to_all(queries, "head", split_axis=1, concat_axis=0, tiled=True),
        lax.all_to_all(key_rows, "head", split_axis=1, concat_axis=0, tiled=True),
        lax.all_to_all(value_rows, "head", split_axis=1, concat_axis=0, tiled=True),
    )
    row_count = head_queries.shape[0]
    group_size = HEADS // KV_HEADS
    local_heads = head_keys.shape[1] // HEAD_DIM
    grouped = head_queries.reshape(row_count, local_heads, group_size, HEAD_DIM)
    cycle_index = lax.axis_index("blk")
    score_scale = HEAD_DIM ** (-0.5)
    my_span = span_of(jnp.full((1,), cycle_index, jnp.int32), span_order)[0]
    query_pos = my_span * row_count + jnp.arange(row_count, dtype=jnp.int32)
    query_visit = jnp.take(visit_ids, query_pos)

    def attend(state_now, kv_block, first_row):
        width = kv_block.shape[1]
        global_rows = first_row + jnp.arange(width, dtype=jnp.int32)
        key_pos = (
            span_of(global_rows // row_count, span_order) * row_count + global_rows % row_count
        )
        key_visit = jnp.take(visit_ids, key_pos)
        allowed = (key_pos[None, :] <= query_pos[:, None]) & (
            key_visit[None, :] == query_visit[:, None]
        )
        run_max, run_total, run_acc = state_now
        key_heads = kv_block[0].reshape(width, local_heads, HEAD_DIM)
        value_heads = kv_block[1].reshape(width, local_heads, HEAD_DIM)
        scores = (
            jnp.einsum("qhgd,khd->qhgk", grouped, key_heads, preferred_element_type=jnp.float32)
            * score_scale
        )
        mask_wide = allowed[:, None, None, :]
        masked = jnp.where(mask_wide, scores, masked_score)
        new_max = jnp.maximum(run_max, jnp.max(masked, axis=-1))
        factor = jnp.exp(run_max - new_max)
        weights = jnp.where(mask_wide, jnp.exp(masked - new_max[..., None]), 0.0)
        new_total = run_total * factor + jnp.sum(weights, axis=-1)
        new_acc = run_acc * factor[..., None] + jnp.einsum(
            "qhgk,khd->qhgd",
            weights.astype(jnp.bfloat16),
            value_heads,
            preferred_element_type=jnp.float32,
        )
        return (new_max, new_total, new_acc)

    kv_local = jnp.stack([head_keys, head_values])
    stat_shape = (row_count, local_heads, group_size)
    initial = (
        jnp.full(stat_shape, masked_score, jnp.float32),
        jnp.zeros(stat_shape, jnp.float32),
        jnp.zeros(stat_shape + (HEAD_DIM,), jnp.float32),
    )
    part_rows = lax.all_gather(kv_local, "blk", axis=1, tiled=True)
    width = part_rows.shape[1]
    step_rows = width
    step_rows = 4 * row_count

    def inner(turn_index, state_in):
        offset = turn_index * step_rows
        sub_block = lax.dynamic_slice_in_dim(part_rows, offset, step_rows, 1)
        return attend(state_in, sub_block, offset)

    state_now = lax.fori_loop(0, width // step_rows, inner, initial)
    run_max, run_total, run_acc = state_now
    attended_local = (run_acc / run_total[..., None]).astype(jnp.bfloat16)
    attended_local = attended_local.reshape(row_count, local_heads * group_size * HEAD_DIM)
    return lax.all_to_all(attended_local, "head", split_axis=0, concat_axis=1, tiled=True)


def fused_kernel(
    dims, q_ref, k_ref, v_ref, visit_ref, span_ref, out_ref,
    kv, qs, outs, bias,
    kv_recv, side_recv, y_send, core_send, z_send, side_send, x_send, x_recv, own_sem, out_send, out_recv, out_own,
):
    nz, nh, rows, phases = dims
    nblk = 4 * nz
    block = nh * rows
    keys = nblk * block
    me = lax.axis_index("blk")
    x = lax.axis_index("head")
    z, y, core = me // 4, (me // 2) % 2, me % 2

    def index_of(z_at, y_at, core_at):
        return z_at * 4 + y_at * 2 + core_at

    y_id = index_of(z, 1 - y, core)
    core_id = index_of(z, y, 1 - core)
    x_peers = [lax.rem(x + step, nh) for step in range(1, nh)]
    side_rows = max(16, block // (2 * (nz - 1)) // 16 * 16)

    def next_plane(up):
        return z + 1 if up else z - 1

    def has_next(up):
        return z + 1 < nz if up else z > 0

    barrier = pltpu.get_barrier_semaphore()
    for blk in (y_id, core_id):
        pl.semaphore_signal(barrier, inc=1, device_id=(blk, x), device_id_type=MESH)
    for xp in x_peers:
        pl.semaphore_signal(barrier, inc=1, device_id=(me, xp), device_id_type=MESH)
    for up in (True, False):

        @pl.when(has_next(up))
        def _(up=up):
            target = index_of(next_plane(up), y, core)
            pl.semaphore_signal(barrier, inc=1, device_id=(target, x), device_id_type=MESH)

    def sources(p, to):
        kv_at = pl.multiple_of((to * phases + p) * HEAD_DIM, HEAD_DIM)
        q_at = pl.multiple_of((to * phases + p) * GROUP * HEAD_DIM, GROUP * HEAD_DIM)
        return (
            k_ref.at[:, pl.ds(kv_at, HEAD_DIM)],
            v_ref.at[:, pl.ds(kv_at, HEAD_DIM)],
            q_ref.at[:, pl.ds(q_at, GROUP * HEAD_DIM)],
        )

    def landing(p, source):
        row = pl.multiple_of(me * block + source * rows, 16)
        return (
            kv.at[p, 0, pl.ds(row, rows), :],
            kv.at[p, 1, pl.ds(row, rows), :],
            qs.at[p, source],
        )

    def own_copies(p, kinds=3, first_kind=0):
        pairs = list(zip(sources(p, x), landing(p, x)))
        return [
            pltpu.make_async_copy(*pairs[kind], own_sem.at[p, kind])
            for kind in range(first_kind, kinds)
        ]

    def x_copies(p, kinds):
        result = []
        for step, xp in enumerate(x_peers):
            from_refs, to_refs = sources(p, xp), landing(p, x)
            for kind in kinds:
                result.append(
                    pltpu.make_async_remote_copy(
                        src_ref=from_refs[kind], dst_ref=to_refs[kind],
                        send_sem=x_send.at[p, step, kind], recv_sem=x_recv.at[p, step, kind],
                        device_id=(me, xp), device_id_type=MESH,
                    )
                )
        return result

    def rows_ref(p, blk, first_row, count):
        at = pl.multiple_of(blk * block + first_row, 16)
        return kv.at[p, :, pl.ds(at, count), :]

    def remote(ref, send_sem, recv_sem, target):
        return pltpu.make_async_remote_copy(
            src_ref=ref, dst_ref=ref, send_sem=send_sem, recv_sem=recv_sem,
            device_id=(target, x), device_id_type=MESH,
        )

    def whole_copy(p, blk, send_sem, target):
        return remote(rows_ref(p, blk, 0, block), send_sem, kv_recv.at[p, blk], target)

    def y_copy(p, plane):
        blk = index_of(plane, y, core)
        if plane is z:
            return whole_copy(p, blk, y_send.at[p, plane], y_id)
        ref = rows_ref(p, blk, side_rows, block - side_rows)
        return remote(ref, y_send.at[p, plane], kv_recv.at[p, blk], y_id)

    def core_copy(p, plane, side):
        blk = index_of(plane, y if side == 0 else 1 - y, core)
        return whole_copy(p, blk, core_send.at[p, side, plane], core_id)

    def z_copy(p, plane, up):
        blk, to = index_of(plane, y, core), index_of(next_plane(up), y, core)
        return whole_copy(p, blk, z_send.at[p, int(up), plane], to)

    def side_copy(p, plane, up):
        blk, to = index_of(plane, 1 - y, core), index_of(next_plane(up), y, core)
        ref = rows_ref(p, blk, 0, side_rows)
        return remote(ref, side_send.at[p, int(up), plane], side_recv.at[p, plane], to)

    def await_whole(p, blk):
        whole_copy(p, blk, y_send.at[p, 0], y_id).wait_recv()

    def for_next(make, act):
        for up in (True, False):
            pl.when(has_next(up))(functools.partial(lambda up: act(make(up)), up))

    def start(copy):
        copy.start()

    def finish(copy):
        copy.wait_send()

    def start_own(p):
        for copy in own_copies(p, 2):
            copy.wait()
        for copy in x_copies(p, (0, 1)):
            copy.wait()
        y_copy(p, z).start()
        for_next(lambda up: z_copy(p, z, up), start)
        core_copy(p, z, 0).start()

    def pass_peer(p):
        await_whole(p, index_of(z, 1 - y, core))
        for_next(lambda up: side_copy(p, z, up), start)
        core_copy(p, z, 1).start()

    def from_planes(distance, act):
        for up in (True, False):
            plane = z - distance if up else z + distance
            exists = plane >= 0 if up else plane < nz
            pl.when(exists)(functools.partial(act, plane, up))

    def pass_plane(p, distance):
        def act(plane, up):
            await_whole(p, index_of(plane, y, core))

            @pl.when(has_next(up))
            def _():
                z_copy(p, plane, up).start()

            y_copy(p, plane).start()
            core_copy(p, plane, 0).start()
            remote(
                rows_ref(p, index_of(plane, 1 - y, core), 0, side_rows),
                side_send.at[p, 0, 0], side_recv.at[p, plane], y_id,
            ).wait_recv()

            @pl.when(has_next(up))
            def _():
                side_copy(p, plane, up).start()

        from_planes(distance, act)

    def finish_plane(p, distance):
        def act(plane, up):
            @pl.when(has_next(up))
            def _():
                z_copy(p, plane, up).wait_send()
                side_copy(p, plane, up).wait_send()

            y_copy(p, plane).wait_send()
            core_copy(p, plane, 0).wait_send()

        from_planes(distance, act)

    def plane_at(rank):
        return lax.rem(z + jnp.where(2 * z < nz, rank, nz - rank), nz)

    def pass_far(p, rank):
        plane = plane_at(rank)
        blk = index_of(plane, 1 - y, core)
        remote(
            rows_ref(p, blk, side_rows, block - side_rows),
            y_send.at[p, 0], kv_recv.at[p, blk], y_id,
        ).wait_recv()
        core_copy(p, plane, 1).start()

    for p in range(phases):
        for copy in own_copies(p):
            copy.start()

    columns = GROUP * block
    column = lax.broadcasted_iota(jnp.int32, (1, columns), 1)
    offset = column
    for g in range(1, GROUP):
        offset = jnp.where(column >= g * block, column - g * block, offset)
    query_pos = span_ref[me] * block + offset
    first = jnp.zeros((1, columns), jnp.int32)
    visits = visit_ref[...]
    for visit in range(1, VISITS):
        begin = jnp.sum(jnp.where(visits < visit, 1.0, 0.0), axis=1, keepdims=True)
        begin = jnp.sum(begin, axis=0, keepdims=True).astype(jnp.int32)
        first = jnp.where(begin <= query_pos, jnp.maximum(first, begin), first)
    row = lax.broadcasted_iota(jnp.int32, (block, 1), 0)

    def mask_block(blk, carry):
        key_pos = span_ref[blk] * block + row
        allowed = (key_pos <= query_pos) & (key_pos >= first)
        bias[pl.ds(pl.multiple_of(blk * block, 16), block), :] = jnp.where(allowed, 0.0, -jnp.inf)
        return carry

    planes_beside = jnp.minimum(z, 1) + jnp.minimum(nz - 1 - z, 1)
    pl.semaphore_wait(barrier, 1 + nh + planes_beside)

    def start_x(p, kinds):
        for copy in x_copies(p, kinds):
            copy.start()

    chunk = 2 * block
    batch = GROUP
    scale = HEAD_DIM**-0.5 * LOG2E
    lowest = -3.0e38

    def compute(p, events):
        at = 0
        query = jnp.concatenate(
            [
                jnp.concatenate([qs[p, h, :, g * HEAD_DIM : (g + 1) * HEAD_DIM] for h in range(nh)], axis=0)
                for g in range(at, at + batch)
            ],
            axis=0,
        )

        query_t = jnp.transpose(query)

        def step(index, state):
            for slot, event in events:
                pl.when(index == slot)(event)
            run_max, run_acc = state
            starts = []
            for rank in (2 * index, 2 * index + 1):
                plane = plane_at(lax.rem(rank, nz))
                chip = plane * 2 + jnp.where(rank < nz, y, 1 - y)
                await_whole(p, chip * 2 + 1 - core)
                starts.append(pl.multiple_of(chip * chunk, 128))
            key = jnp.concatenate([kv[p, 0, pl.ds(at, chunk), :] for at in starts], axis=0)
            value = jnp.concatenate([kv[p, 1, pl.ds(at, chunk), :] for at in starts], axis=0)
            mask = jnp.concatenate([bias[pl.ds(at, chunk), :] for at in starts], axis=0)
            extended = jnp.concatenate(
                [jnp.transpose(value), jnp.ones((16, 2 * chunk), jnp.bfloat16)], axis=0
            )
            score = jnp.dot(key, query_t, preferred_element_type=jnp.float32)
            shifted = score * scale + mask
            new_max = jnp.maximum(run_max, jnp.max(shifted, axis=0, keepdims=True))
            weight = jnp.exp2(shifted - new_max).astype(jnp.bfloat16)
            factor = jnp.exp2(run_max - new_max)
            new_acc = run_acc * factor + jnp.dot(
                extended, weight, preferred_element_type=jnp.float32
            )
            return new_max, new_acc

        initial = (
            jnp.full((1, columns), lowest, jnp.float32),
            jnp.zeros((HEAD_DIM + 16, columns), jnp.float32),
        )
        _, acc = lax.fori_loop(0, nz, step, initial)
        result = jnp.transpose(acc[:HEAD_DIM] / acc[HEAD_DIM : HEAD_DIM + 1]).astype(jnp.bfloat16)
        for i in range(batch):
            for h in range(nh):
                first_row = i * block + h * rows
                outs[p, h, :, (at + i) * HEAD_DIM : (at + i + 1) * HEAD_DIM] = result[
                    first_row : first_row + rows
                ]

    width = GROUP * HEAD_DIM

    def out_copies(p):
        place = out_ref.at[:, pl.ds(pl.multiple_of((x * phases + p) * width, width), width)]
        copies = [pltpu.make_async_copy(outs.at[p, x], place, out_own.at[p])]
        for step, xp in enumerate(x_peers):
            copies.append(
                pltpu.make_async_remote_copy(
                    src_ref=outs.at[p, xp], dst_ref=place,
                    send_sem=out_send.at[p, step], recv_sem=out_recv.at[p, step],
                    device_id=(me, xp), device_id_type=MESH,
                )
            )
        return copies

    def events_of(p):
        events = []
        for rank in range(1, nz):
            events.append((min(rank, nz - 2), functools.partial(pass_far, p, rank)))
        if p + 1 < phases:
            events.append((0, functools.partial(pass_peer, p + 1)))
            for distance in range(1, nz):
                events.append((distance, functools.partial(pass_plane, p + 1, distance)))
        return events

    start_x(0, (0, 1))
    lax.fori_loop(0, nblk, mask_block, 0)
    start_own(0)
    for p in range(1, min(2, phases)):
        start_x(p, (0, 1))
        start_own(p)
        start_x(p - 1, (2,))
    pass_peer(0)
    for p in range(min(2, phases), min(3, phases)):
        start_x(p, (0, 1))
    start_x(min(2, phases) - 1, (2,))
    for distance in range(1, nz):
        pass_plane(0, distance)
    for p in range(phases):
        if p + 2 < phases:
            start_own(p + 2)
            start_x(p + 2, (2,))
            if p + 3 < phases:
                start_x(p + 3, (0, 1))
        for copy in own_copies(p, 3, 2):
            copy.wait()
        for copy in x_copies(p, (2,)):
            copy.wait()
        compute(p, events_of(p))
        for copy in out_copies(p):
            copy.start()
    for p in range(phases):
        for copy in out_copies(p):
            copy.wait()
        y_copy(p, z).wait_send()
        for_next(lambda up: z_copy(p, z, up), finish)
        for_next(lambda up: side_copy(p, z, up), finish)
        for side in range(2):
            core_copy(p, z, side).wait_send()
        for distance in range(1, nz):
            finish_plane(p, distance)
            core_copy(p, plane_at(distance), 1).wait_send()


def fused_body(nblk, nh, queries, key_rows, value_rows, visit_ids, span_order):
    rows = queries.shape[0]
    block = rows * nh
    phases = KV_HEADS // nh
    nz = nblk // 4
    dma = pltpu.SemaphoreType.DMA
    any_spec = pl.BlockSpec(memory_space=pl.ANY)
    return pl.pallas_call(
        functools.partial(fused_kernel, (nz, nh, rows, phases)),
        out_shape=jax.ShapeDtypeStruct(queries.shape, jnp.bfloat16),
        in_specs=[
            any_spec,
            any_spec,
            any_spec,
            pl.BlockSpec(memory_space=pltpu.VMEM),
            pl.BlockSpec(memory_space=pltpu.SMEM),
        ],
        out_specs=any_spec,
        scratch_shapes=[
            pltpu.VMEM((phases, 2, nblk * block, HEAD_DIM), jnp.bfloat16),
            pltpu.VMEM((phases, nh, rows, GROUP * HEAD_DIM), jnp.bfloat16),
            pltpu.VMEM((phases, nh, rows, GROUP * HEAD_DIM), jnp.bfloat16),
            pltpu.VMEM((nblk * block, GROUP * block), jnp.float32),
            dma((phases, nblk)),
            dma((phases, nz)),
            dma((phases, nz)),
            dma((phases, 2, nz)),
            dma((phases, 2, nz)),
            dma((phases, 2, nz)),
            dma((phases, nh - 1, 3)),
            dma((phases, nh - 1, 3)),
            dma((phases, 3)),
            dma((phases, nh - 1)),
            dma((phases, nh - 1)),
            dma((phases,)),
        ],
        compiler_params=pltpu.CompilerParams(
            collective_id=0, has_side_effects=True, vmem_limit_bytes=60 * 2**20
        ),
        name="visit_attention",
    )(queries, key_rows, value_rows, visit_ids.reshape(-1, 128), span_order)


def solution(mesh):
    placed = (
        P(("blk", "head"), None),
        P(("blk", "head"), None),
        P(("blk", "head"), None),
        P(),
        P(),
    )
    nblk, nh = mesh.shape["blk"], mesh.shape["head"]

    def body(queries, *rest):
        if queries.shape[0] % 16 == 0 and nblk % 8 == 0 and KV_HEADS % nh == 0:
            return fused_body(nblk, nh, queries, *rest)
        return gathered_body(queries, *rest)

    return jax.shard_map(
        body, mesh=mesh, in_specs=placed, out_specs=P(("blk", "head"), None), check_vma=False
    )
```
